32 devices in a mesh: section: 2 (over x), dp: 4 (over y, core), seq: 4 (over z).
Axes of the slice: x: 2, y: 2, z: 4, core: 2. Of those that a mesh axis runs over, the one named last changes fastest.
Arguments:
- tokens: bfloat16 [2, 4, 1024, 768], P(None, 'dp', 'seq'), may hold values from -6 to 6
- cotangent: bfloat16 [2, 4, 1024, 768], P(None, 'dp', 'seq'), may hold values from -6 to 6
- in_weight: bfloat16 [2, 768, 3352], P('section', ('dp', 'seq')), may hold values from -0.21875 to 0.21875
- out_weight: bfloat16 [2, 1536, 768], P('section', ('dp', 'seq')), may hold values from -0.15625 to 0.15625
- conv_weight: bfloat16 [2, 4, 1792], P('section', None, ('dp', 'seq')), may hold values from -3 to 3
- conv_bias: bfloat16 [2, 1792], P('section', ('dp', 'seq')), may hold values from -2.5 to 2.5
- norm_gain: bfloat16 [2, 768], P('section', ('dp', 'seq')), may hold values from 0.25 to 1.75
- gate_gain: bfloat16 [2, 1536], P('section', ('dp', 'seq')), may hold values from 0.25 to 1.75
- dt_bias: float32 [2, 24], P('section'), may hold values from -6 to -3.5
- a_log: float32 [2, 24], P('section'), as said below
- d_skip: float32 [2, 24], P('section'), may hold values from 0.5 to 1.5
Outputs:
- activations: bfloat16 [2, 2, 4, 1024, 768], P('section', None, 'dp', 'seq')
- input_grads: float32 [2, 2, 4, 1024, 768], P('section', None, 'dp', 'seq')
- in_weight_grad: float32 [2, 768, 3352], P('section', ('dp', 'seq'))
- out_weight_grad: float32 [2, 1536, 768], P('section', ('dp', 'seq'))
- conv_weight_grad: float32 [2, 4, 1792], P('section', None, ('dp', 'seq'))
- conv_bias_grad: float32 [2, 1792], P('section', ('dp', 'seq'))
- norm_gain_grad: float32 [2, 768], P('section', ('dp', 'seq'))
- gate_gain_grad: float32 [2, 1536], P('section', ('dp', 'seq'))
- dt_bias_grad: float32 [2, 24], P('section')
- a_log_grad: float32 [2, 24], P('section')
- d_skip_grad: float32 [2, 24], P('section')
The draws below stay inside these ranges and needn't reach their ends.
Inputs may be any that keep to these rules, and one draw needn't show every extreme that they name: `a_log`: each head's decay rate, with its step size bias.
All inputs are finite; a program needn't handle non-finite values.
Results may differ from the reference program's by a relative error of at most 0.02.
Values may be sent and summed in bfloat16 or wider, within the bound.
A program may use at most 256 MiB of HBM per device.

```python
import math
import jax
import jax.numpy as jnp
from jax import lax

D = 768
DI = 1536
P_SIZE = 64
N = 128
CONVK = 4
GROUP = 256
MB = 2
H = 24
CH = 1792
E = 3352
SECTIONS = 2
SEQS = 4
LEN = 1024
N_SEQ = 4


def head_rates(key):
    step_bias = jax.random.uniform(jax.random.fold_in(key, 11), (SECTIONS, H), jnp.float32, -6.0, -3.5)
    fraction = jax.random.uniform(jax.random.fold_in(key, 12), (SECTIONS, H), jnp.float32)
    return (step_bias, fraction)


def draw_dt_bias(key, part):
    step_bias, fraction = head_rates(key)
    return step_bias


def draw_a_log(key, part):
    step_bias, fraction = head_rates(key)
    block_rate = math.log(0.15) + fraction * (math.log(3.0) - math.log(0.15))
    return block_rate - math.log(GROUP) - (step_bias + 0.5)


def block_levels(own_key, extent, shards, low, top_value):
    def one(position, parts):
        heights = jax.random.uniform(jax.random.fold_in(jax.random.fold_in(own_key, 6), position), (parts,), jnp.float32, low / len(shards), top_value / len(shards))
        return jnp.repeat(jnp.exp(heights), extent[position] // parts).reshape((-1,) + (1,) * (len(extent) - position - 1))

    level = one(*shards[0])
    for cut in shards[1:]:
        level = level * one(*cut)
    return level


def centred(key, extent, deviation, bound, split=(), held_as=jnp.bfloat16):
    values = jax.random.normal(key, extent, jnp.float32) * deviation
    if len(split) > 0:
        values = block_levels(key, extent, split, -0.22, 0.18) * values
    return jnp.clip(values, min=-bound, max=bound).astype(held_as)


def setup_inputs(seed: int = 0) -> dict:
    arg_keys = jax.random.split(jax.random.key(seed), 12)
    return {
        "tokens": centred(arg_keys[0], (MB, SEQS, LEN, D), 1.0, 6.0, ((1, 4), (2, 4))),
        "cotangent": centred(arg_keys[1], (MB, SEQS, LEN, D), 1.0, 6.0, ((1, 4), (2, 4))),
        "in_weight": centred(arg_keys[2], (SECTIONS, D, E), D ** -0.5, 0.21875, ((0, 2), (1, 16))),
        "out_weight": centred(arg_keys[3], (SECTIONS, DI, D), DI ** -0.5, 0.15625, ((0, 2), (1, 16))),
        "conv_weight": centred(arg_keys[4], (SECTIONS, CONVK, CH), CONVK ** -0.5, 3.0, ((0, 2), (2, 16))),
        "conv_bias": centred(arg_keys[5], (SECTIONS, CH), 0.3, 2.5, ((0, 2), (1, 16))),
        "norm_gain": jnp.clip(1.0 + 0.15 * jax.random.normal(arg_keys[6], (SECTIONS, D), jnp.float32), 0.25, 1.75).astype(jnp.bfloat16),
        "gate_gain": jnp.clip(1.0 + 0.15 * jax.random.normal(arg_keys[7], (SECTIONS, DI), jnp.float32), 0.25, 1.75).astype(jnp.bfloat16),
        "dt_bias": draw_dt_bias(jax.random.fold_in(arg_keys[11], 71), 0),
        "a_log": draw_a_log(jax.random.fold_in(arg_keys[11], 71), 0),
        "d_skip": jnp.clip(0.5 + 1.0 * jax.random.uniform(arg_keys[10], (SECTIONS, H), jnp.float32) ** block_levels(arg_keys[10], (SECTIONS, H), ((0, 2),), -0.2, 0.2), 0.5, 1.5),
    }


@jax.custom_vjp
def low(v):
    return lax.optimization_barrier(v.astype(jnp.bfloat16)).astype(jnp.float32)

@jax.custom_vjp
def low_back(v):
    return v

def low_keep(v):
    return (low(v), None)

def low_pass(kept, grad):
    return (grad,)

def back_keep(v):
    return (v, None)

def back_low(kept, grad):
    return (low(grad),)
low.defvjp(low_keep, low_pass)
low_back.defvjp(back_keep, back_low)
EPSILON = 1e-05
PRECISE = lax.Precision.HIGHEST

def matmul_hi(left, right):
    return jnp.dot(left, right, precision=PRECISE)

def rms_scale(values, gain):
    return values * lax.rsqrt(lax.optimization_barrier(jnp.mean(values * values, axis=-1, keepdims=True)) + EPSILON) * gain

def mamba_layer(layer_in, params):
    w_in, w_out, conv_w, conv_b, gain_n, gain_g, dt_bias, a_log, d_skip = params
    normed = low(rms_scale(layer_in, gain_n))
    projected = low(low_back(matmul_hi(normed, w_in)))
    gate_cols = projected[:, :DI]
    conv_in = projected[:, DI:DI + CH]
    dt_raw = projected[:, DI + CH:]
    padded = jnp.concatenate([jnp.zeros((CONVK - 1, CH), jnp.float32), conv_in], axis=0)
    conv_out = conv_b
    for k in range(CONVK):
        conv_out = conv_out + conv_w[k] * padded[k:k + LEN]
    activated = low(jax.nn.silu(conv_out))
    heads_x = activated[:, :DI].reshape(N_SEQ, GROUP, H, P_SIZE)
    b_proj = activated[:, DI:DI + N].reshape(N_SEQ, GROUP, N)
    c_proj = activated[:, DI + N:].reshape(N_SEQ, GROUP, N)
    dt_step = jax.nn.softplus(dt_raw + dt_bias).reshape(N_SEQ, GROUP, H)
    cumulative = jnp.cumsum(dt_step * -jnp.exp(a_log), axis=1)
    causal_mask = jnp.tril(jnp.ones((GROUP, GROUP), jnp.bool_))[None, :, :, None]
    log_gap = cumulative[:, :, None, :] - cumulative[:, None, :, :]
    decay_mat = jnp.where(causal_mask, jnp.exp(jnp.where(causal_mask, log_gap, 0.0)), 0.0)
    inner_cb = jnp.einsum('ctn,csn->cts', c_proj, b_proj, precision=PRECISE)
    mixing = low(inner_cb[..., None] * decay_mat * dt_step[:, None, :, :])
    y_intra = jnp.einsum('ctsh,cshp->cthp', mixing, heads_x, precision=PRECISE)
    to_end = jnp.exp(cumulative[:, -1:, :] - cumulative)
    weighted = low(heads_x * (dt_step * to_end)[..., None])
    states = low_back(jnp.einsum('cshp,csn->chpn', weighted, b_proj, precision=PRECISE))
    totals = jnp.exp(cumulative[:, -1, :])

    def carry_state(held_state, block_item):
        total, state = block_item
        return (total[:, None, None] * held_state + state, held_state)
    _, incoming = lax.scan(carry_state, jnp.zeros((H, P_SIZE, N), jnp.float32), (totals, states))
    c_decayed = low(c_proj[:, :, None, :] * jnp.exp(cumulative)[..., None])
    y_inter = jnp.einsum('cthn,chpn->cthp', c_decayed, low(incoming), precision=PRECISE)
    y_out = low_back(y_intra + y_inter + d_skip[:, None] * heads_x).reshape(LEN, DI)
    gated_y = y_out * jax.nn.silu(gate_cols)
    normed_out = low(rms_scale(gated_y, gain_g))
    return layer_in + low_back(matmul_hi(normed_out, w_out))

def reference(tokens, cotangent, in_weight, out_weight, conv_weight, conv_bias, norm_gain, gate_gain, dt_bias, a_log, d_skip):
    weights = tuple((w.astype(jnp.float32) for w in (in_weight, out_weight, conv_weight, conv_bias, norm_gain, gate_gain, dt_bias, a_log, d_skip)))
    seq_tokens = tokens.astype(jnp.float32).reshape(MB * SEQS, LEN, D)
    probe_terms = jnp.zeros((MB * SEQS, SECTIONS, LEN, D), jnp.float32)

    def forward(seq_tokens, probe_terms, weights):

        def run_sequence(block_item):
            stream, probes = block_item
            outputs = []
            for layer_idx in range(SECTIONS):
                if layer_idx > 0:
                    stream = low(low_back(stream))
                stream = mamba_layer(stream + probes[layer_idx], tuple((w[layer_idx] for w in weights)))
                outputs.append(stream)
            return jnp.stack(outputs)
        return lax.map(jax.checkpoint(run_sequence), (seq_tokens, probe_terms))
    layer_outs, pullback = jax.vjp(forward, seq_tokens, probe_terms, weights)
    cot_full = jnp.zeros_like(layer_outs).at[:, SECTIONS - 1].set(cotangent.astype(jnp.float32).reshape(MB * SEQS, LEN, D))
    _, probe_grads, weight_grads = pullback(cot_full)

    def arrange(values):
        return jnp.transpose(values.reshape(MB, SEQS, SECTIONS, LEN, D), (2, 0, 1, 3, 4))
    return (arrange(layer_outs).astype(jnp.bfloat16), arrange(probe_grads), weight_grads[0], weight_grads[1], weight_grads[2], weight_grads[3], weight_grads[4], weight_grads[5], weight_grads[6], weight_grads[7], weight_grads[8])
```

```python
import jax
import jax.numpy as jnp
from jax import lax
from jax.experimental import pallas as pl
from jax.experimental.pallas import tpu as pltpu
from jax.sharding import PartitionSpec as P

D = 768
DI = 1536
P_SIZE = 64
N = 128
CONVK = 4
MB = 2
H = 24
CH = 1792
E = 3352
PAIRS = H // 2
PAIR = 2 * P_SIZE
EDGE = 16

EPSILON = 1e-05
PRECISE = lax.Precision.HIGHEST
f32 = jnp.float32
bf16 = jnp.bfloat16
WEIGHT_AXES = ("dp", "seq")


def dot(left, right, dims=((1,), (0,)), precision=None):
    return lax.dot_general(left, right, (dims, ((), ())), preferred_element_type=f32, precision=precision)


def rows_dot(left, right, precision=None):
    return dot(left, right, ((0,), (0,)), precision)


def cols_dot(left, right, precision=None):
    return dot(left, right, ((1,), (1,)), precision)


def shifted(x, axis, by):
    length = lax.axis_size(axis)
    pairs = [(i, i + by) for i in range(length) if 0 <= i + by < length]
    return lax.ppermute(x, axis, pairs)


def swapped(x):
    return lax.ppermute(x, "section", [(0, 1), (1, 0)])


def head_matrix():
    rows = lax.broadcasted_iota(jnp.int32, (H, DI), 0)
    cols = lax.broadcasted_iota(jnp.int32, (H, DI), 1)
    return (rows == cols // P_SIZE).astype(f32)


def expand(values):
    return dot(values, head_matrix(), precision=PRECISE)


def head_sums(values):
    return cols_dot(values, head_matrix(), precision=PRECISE)


def silu_slope(values):
    sigma = jax.nn.sigmoid(values)
    return sigma * (1.0 + values * (1.0 - sigma))


def lower_half(shape):
    return lax.broadcasted_iota(jnp.int32, shape, 1) < P_SIZE


def causal_decay(col, row):
    rows = col.shape[0]
    mask = lax.broadcasted_iota(jnp.int32, (rows, rows), 0) >= lax.broadcasted_iota(
        jnp.int32, (rows, rows), 1
    )
    return jnp.exp(jnp.where(mask, col - row, -1e30))


def intra_kernel(x_ref, b_ref, c_ref, cum_ref, cumt_ref, dtt_ref, skip_ref, y_ref, cb_ref):
    @pl.when(pl.program_id(0) == 0)
    def _():
        cb_ref[...] = cols_dot(c_ref[...], b_ref[...])

    x = x_ref[...]
    parts = []
    for i in range(2):
        decay = causal_decay(cum_ref[:, i * P_SIZE : i * P_SIZE + 1], cumt_ref[0, i : i + 1, :])
        mix = (cb_ref[...] * decay * dtt_ref[0, i : i + 1, :]).astype(bf16)
        parts.append(dot(mix, x))
    y = jnp.where(lower_half(x.shape), parts[0], parts[1])
    y_ref[...] = y + skip_ref[...] * x.astype(f32)


def inter_kernel(c_ref, cum_ref, held_ref, part_ref, y_ref):
    c = c_ref[...].astype(f32)
    parts = []
    for i in range(2):
        cdec = (c * jnp.exp(cum_ref[:, i * P_SIZE : i * P_SIZE + 1])).astype(bf16)
        parts.append(dot(cdec, held_ref[...]))
    y_ref[...] = part_ref[...] + jnp.where(lower_half(parts[0].shape), parts[0], parts[1])


def held_grad_kernel(c_ref, cum_ref, dy_ref, out_ref):
    c = c_ref[...].astype(f32)
    parts = []
    for i in range(2):
        cdec = (c * jnp.exp(cum_ref[:, i * P_SIZE : i * P_SIZE + 1])).astype(bf16)
        parts.append(rows_dot(cdec, dy_ref[...]))
    out_ref[...] = jnp.where(lower_half(parts[0].shape), parts[0], parts[1])


def mix_grad_kernel(
    dy_ref,
    x_ref,
    b_ref,
    c_ref,
    cum_ref,
    cumt_ref,
    dtt_ref,
    held_ref,
    skip_ref,
    dx_ref,
    dstep_ref,
    dcum_ref,
    db_ref,
    dc_ref,
    cb_ref,
    dcb_ref,
):
    step = pl.program_id(0)

    @pl.when(step == 0)
    def _():
        cb_ref[...] = cols_dot(c_ref[...], b_ref[...])
        dcb_ref[...] = jnp.zeros_like(dcb_ref)
        dc_ref[...] = jnp.zeros_like(dc_ref)
        dcum_ref[...] = jnp.zeros_like(dcum_ref)

    dy = dy_ref[...]
    x = x_ref[...]
    c = c_ref[...].astype(f32)
    low = lower_half(dy.shape)
    lane = lax.broadcasted_iota(jnp.int32, dcum_ref.shape, 1)
    dx_parts = []
    for i in range(2):
        cum_col = cum_ref[:, i * P_SIZE : i * P_SIZE + 1]
        dt_row = dtt_ref[0, i : i + 1, :]
        decay = causal_decay(cum_col, cumt_ref[0, i : i + 1, :])
        cb_decay = cb_ref[...] * decay
        mix = (cb_decay * dt_row).astype(bf16)
        dx_parts.append(rows_dot(mix, dy))
        own = jnp.where(low if i == 0 else jnp.logical_not(low), dy, jnp.zeros_like(dy))
        dmix = cols_dot(own, x)
        dcb_ref[...] += dmix * decay * dt_row
        inner = dmix * cb_decay
        dstep_ref[0, i : i + 1, :] = jnp.sum(inner, axis=0, keepdims=True)
        grow = jnp.sum(inner * dt_row, axis=1, keepdims=True)
        dcdec = cols_dot(own, held_ref[...])
        grown = dcdec * jnp.exp(cum_col)
        dc_ref[...] += grown
        grow = grow + jnp.sum(grown * c, axis=1, keepdims=True)
        dcum_ref[...] += jnp.where(lane == 2 * step + i, grow, 0.0)
    dx_ref[...] = jnp.where(low, dx_parts[0], dx_parts[1]) + skip_ref[...] * dy.astype(f32)

    @pl.when(step == PAIRS - 1)
    def _():
        dc_ref[...] += dot(dcb_ref[...], b_ref[...].astype(f32), precision=PRECISE)
        db_ref[...] = rows_dot(dcb_ref[...], c, precision=PRECISE)


def by_pair(rows):
    return pl.BlockSpec((rows, PAIR), lambda j: (0, j))


def fixed(rows, block):
    return pl.BlockSpec((rows, PAIR), lambda j: (0, block))


def head_rows(rows):
    return pl.BlockSpec((1, 2, rows), lambda j: (j, 0, 0))


def call(kernel, out_shape, in_specs, out_specs, scratch=()):
    return pl.pallas_call(
        kernel,
        grid=(PAIRS,),
        out_shape=out_shape,
        in_specs=in_specs,
        out_specs=out_specs,
        scratch_shapes=list(scratch),
        compiler_params=pltpu.CompilerParams(vmem_limit_bytes=32 * 1024 * 1024),
    )


def shaped(*shape, dtype=f32):
    return jax.ShapeDtypeStruct(shape, dtype)


B_BLOCK = DI // PAIR
C_BLOCK = B_BLOCK + 1


def intra(acts, cum_wide, cum_t, dt_t, skip_wide):
    t = acts.shape[0]
    return call(
        intra_kernel,
        shaped(t, DI),
        [by_pair(t), fixed(t, B_BLOCK), fixed(t, C_BLOCK), by_pair(t), head_rows(t), head_rows(t), by_pair(1)],
        by_pair(t),
        [pltpu.VMEM((t, t), f32)],
    )(acts, acts, acts, cum_wide, cum_t, dt_t, skip_wide)


def inter(acts, cum_wide, held, part):
    t = acts.shape[0]
    return call(
        inter_kernel,
        shaped(t, DI),
        [fixed(t, C_BLOCK), by_pair(t), by_pair(N), by_pair(t)],
        by_pair(t),
    )(acts, cum_wide, held, part)


def held_grad(acts, cum_wide, dy):
    t = acts.shape[0]
    return call(
        held_grad_kernel,
        shaped(N, DI),
        [fixed(t, C_BLOCK), by_pair(t), by_pair(t)],
        by_pair(N),
    )(acts, cum_wide, dy)


def mix_grad(dy, acts, cum_wide, cum_t, dt_t, held, skip_wide):
    t = acts.shape[0]
    return call(
        mix_grad_kernel,
        (shaped(t, DI), shaped(PAIRS, 2, t), shaped(t, PAIR), shaped(t, N), shaped(t, N)),
        [
            by_pair(t),
            by_pair(t),
            fixed(t, B_BLOCK),
            fixed(t, C_BLOCK),
            by_pair(t),
            head_rows(t),
            head_rows(t),
            by_pair(N),
            by_pair(1),
        ],
        (by_pair(t), head_rows(t), fixed(t, 0), fixed(t, 0), fixed(t, 0)),
        [pltpu.VMEM((t, t), f32), pltpu.VMEM((t, t), f32)],
    )(dy, acts, acts, acts, cum_wide, cum_t, dt_t, held, skip_wide)


def lower_triangle(rows):
    return (
        lax.broadcasted_iota(jnp.int32, (rows, rows), 0)
        >= lax.broadcasted_iota(jnp.int32, (rows, rows), 1)
    ).astype(f32)


def rms_parts(values):
    inv_rms = lax.rsqrt(jnp.mean(values * values, axis=-1, keepdims=True) + EPSILON)
    return inv_rms, values * inv_rms


def layer_forward(layer_in, weights):
    w_in, w_out, conv_w, conv_b, norm_g, gate_g, bias_dt, log_rate, skip_gain = weights
    t = layer_in.shape[0]
    _, normed = rms_parts(layer_in.astype(f32))
    projected = dot((normed * norm_g).astype(bf16), w_in).astype(bf16)
    xbc = projected[:, DI : DI + CH]
    edge = shifted(xbc[t - EDGE :], "seq", 1)
    padded = jnp.concatenate([edge[EDGE - CONVK + 1 :], xbc], axis=0)
    conv = conv_b
    for k in range(CONVK):
        conv = conv + conv_w[k : k + 1] * padded[k : k + t].astype(f32)
    acts = jax.nn.silu(conv).astype(bf16)
    dt = jax.nn.softplus(projected[:, DI + CH :].astype(f32) + bias_dt)
    cum = dot(lower_triangle(t), dt * -jnp.exp(log_rate), precision=PRECISE)
    to_end = jnp.exp(cum[-1:] - cum)
    factor_wide = expand(dt * to_end)
    weighted = (acts[:, :DI].astype(f32) * factor_wide).astype(bf16)
    states = rows_dot(acts[:, DI : DI + N], weighted)
    totals = jnp.exp(cum[-1:])
    totals_wide = expand(totals)
    incoming = shifted(states.astype(bf16), "seq", 1)
    for _ in range(lax.axis_size("seq") - 2):
        incoming = shifted((totals_wide * incoming.astype(f32) + states).astype(bf16), "seq", 1)
    cum_wide = expand(cum)
    cum_t = cum.T.reshape(PAIRS, 2, t)
    dt_t = dt.T.reshape(PAIRS, 2, t)
    skip_wide = expand(skip_gain)
    part = intra(acts, cum_wide, cum_t, dt_t, skip_wide)
    y = inter(acts, cum_wide, incoming, part)
    gate_cols = projected[:, :DI].astype(f32)
    _, q = rms_parts(y * jax.nn.silu(gate_cols))
    mixed = layer_in.astype(f32) + dot((q * gate_g).astype(bf16), w_out)
    kept = (layer_in, projected, padded, acts, conv, dt, cum, cum_wide, cum_t, dt_t, skip_wide, incoming, y, weighted, factor_wide, totals, totals_wide)
    return mixed.astype(bf16), kept


def layer_backward(grad_v, kept, weights):
    w_in, w_out, conv_w, conv_b, norm_g, gate_g, bias_dt, log_rate, skip_gain = weights
    (layer_in, projected, padded, acts, conv, dt, cum, cum_wide, cum_t, dt_t, skip_wide, incoming, y, weighted, factor_wide, totals, totals_wide) = kept
    t = layer_in.shape[0]
    dob = grad_v.astype(bf16)
    z = projected[:, :DI].astype(f32)
    swish = jax.nn.silu(z)
    r2, q = rms_parts(y * swish)
    dyn = cols_dot(dob, w_out)
    grad_gate_gain = jnp.sum(dyn * q, axis=0)
    dq = dyn * gate_g
    dgated = r2 * (dq - q * jnp.mean(dq * q, axis=-1, keepdims=True))
    dz = (dgated * y * silu_slope(z)).astype(bf16)
    dy = (dgated * swish).astype(bf16)
    x = acts[:, :DI].astype(f32)
    grad_skip = head_sums(jnp.sum(dy.astype(f32) * x, axis=0, keepdims=True))[0]
    dheld = held_grad(acts, cum_wide, dy)
    leave = shifted(dheld.astype(bf16), "seq", -1)
    for _ in range(lax.axis_size("seq") - 2):
        leave = shifted((totals_wide * leave.astype(f32) + dheld).astype(bf16), "seq", -1)
    grad_wout = rows_dot((q * gate_g).astype(bf16), dob)
    dx, dstep_t, dcum, db, dc = mix_grad(dy, acts, cum_wide, cum_t, dt_t, incoming, skip_wide)
    dstep = dstep_t.reshape(H, t).T
    dcum = dcum[:, :H] - dstep * dt
    db = db + cols_dot(weighted, leave)
    dweighted = dot(acts[:, DI : DI + N], leave)
    dx = dx + dweighted * factor_wide
    to_end = jnp.exp(cum[-1:] - cum)
    dfactor = head_sums(dweighted * x)
    dstep = dstep + dfactor * to_end
    dend = dfactor * dt * to_end
    at_total = head_sums(jnp.sum(leave.astype(f32) * incoming.astype(f32), axis=0, keepdims=True))
    last = jnp.sum(dend, axis=0, keepdims=True) + at_total * totals
    is_end = lax.broadcasted_iota(jnp.int32, (t, 1), 0) == t - 1
    dcum = dcum - dend + jnp.where(is_end, last, 0.0)
    drate = rows_dot(lower_triangle(t), dcum, precision=PRECISE)
    rates = -jnp.exp(log_rate)
    dstep = dstep + drate * rates
    grad_alog = jnp.sum(drate * dt, axis=0) * rates[0]
    draw = dstep * jax.nn.sigmoid(projected[:, DI + CH :].astype(f32) + bias_dt)
    grad_dtb = jnp.sum(draw, axis=0)
    dconv = jnp.concatenate([dx, db, dc], axis=1) * silu_slope(conv)
    edge = shifted(dconv[:8], "seq", -1)
    grad_cb = jnp.sum(dconv, axis=0)
    grad_cw = jnp.stack([jnp.sum(dconv * padded[k : k + t].astype(f32), axis=0) for k in range(CONVK)])
    ext = jnp.concatenate([dconv, edge[: CONVK - 1]], axis=0)
    dxbc = jnp.zeros((t, CH), f32)
    for k in range(CONVK):
        dxbc = dxbc + conv_w[k : k + 1] * ext[CONVK - 1 - k : CONVK - 1 - k + t]
    dproj = jnp.concatenate([dz, dxbc.astype(bf16), draw.astype(bf16)], axis=1)
    inv_rms, normed = rms_parts(layer_in.astype(f32))
    grad_win = rows_dot((normed * norm_g).astype(bf16), dproj)
    dun = cols_dot(dproj, w_in)
    grad_norm_gain = jnp.sum(dun * normed, axis=0)
    dnorm = dun * norm_g
    grad_u = grad_v.astype(f32) + inv_rms * (dnorm - normed * jnp.mean(dnorm * normed, axis=-1, keepdims=True))
    return grad_u, grad_win, grad_wout, (grad_cw, grad_cb, grad_norm_gain, grad_gate_gain, grad_dtb, grad_alog, grad_skip)


def reduced(grad):
    return lax.psum_scatter(grad.astype(bf16), WEIGHT_AXES, scatter_dimension=0, tiled=True)


def body(tokens, cotangent, in_weight, out_weight, conv_weight, conv_bias, norm_gain, gate_gain, dt_bias, a_log, d_skip):
    first = lax.axis_index("section") == 0
    share_count = lax.axis_size("dp") * lax.axis_size("seq")
    share_idx = lax.axis_index("dp") * lax.axis_size("seq") + lax.axis_index("seq")

    def pick(a, b):
        return jnp.where(first, a, b)

    mine = (in_weight[0], out_weight[0])
    theirs = tuple(swapped(w) for w in mine)
    small = jnp.concatenate([conv_weight[0].reshape(-1), conv_bias[0], norm_gain[0], gate_gain[0]])
    smalls = lax.all_gather(small, ("section",) + WEIGHT_AXES, axis=0, tiled=False)
    smalls = smalls.reshape(2, share_count, small.shape[0]).astype(f32)
    heads = jnp.stack([dt_bias[0], a_log[0], d_skip[0]])
    other_heads = swapped(heads)
    head_params = (pick(heads, other_heads), pick(other_heads, heads))
    c_loc, n_loc, g_loc = conv_bias.shape[1], norm_gain.shape[1], gate_gain.shape[1]
    weights = []
    for layer in range(2):
        shards = tuple(pick(m, o) if layer == 0 else pick(o, m) for m, o in zip(mine, theirs))
        w_in, w_out = (lax.all_gather(s, WEIGHT_AXES, axis=0, tiled=True) for s in shards)
        own = smalls[layer]
        cuts = [0, CONVK * c_loc, CONVK * c_loc + c_loc, CONVK * c_loc + c_loc + n_loc]
        conv_w = own[:, : cuts[1]].reshape(share_count, CONVK, c_loc).transpose(1, 0, 2).reshape(CONVK, CH)
        conv_b = own[:, cuts[1] : cuts[2]].reshape(1, CH)
        norm_g = own[:, cuts[2] : cuts[3]].reshape(1, D)
        gate_g = own[:, cuts[3] :].reshape(1, DI)
        hp = head_params[layer]
        weights.append((w_in, w_out, conv_w, conv_b, norm_g, gate_g, hp[0:1], hp[1:2], hp[2:3]))

    stream = pick(tokens[0, 0], tokens[1, 0])
    acts, kept = [], []
    for layer in range(2):
        stream, saved = layer_forward(stream, weights[layer])
        acts.append(stream)
        kept.append(saved)
    grad = pick(cotangent[0, 0], cotangent[1, 0])
    grads, shares, packs = [None, None], [None, None], [None, None]
    for layer in (1, 0):
        grad, grad_win, grad_wout, rest = layer_backward(grad, kept[layer], weights[layer])
        grads[layer] = grad
        shares[layer] = (reduced(grad_win), reduced(grad_wout))
        packs[layer] = jnp.concatenate([r.reshape(-1) for r in rest])
        grad = grad.astype(bf16)

    def finish(low, high):
        own = pick(low, high)
        return own, swapped(pick(high, low))

    def by_micro(low, high):
        own, other = finish(low, high)
        return jnp.stack([pick(own, other), pick(other, own)])[None, :, None]

    act_out = by_micro(*acts)
    grad_out = by_micro(*grads)
    sums = []
    for low, high in zip(*shares):
        own, other = finish(low, high)
        sums.append((own.astype(f32) + other.astype(f32))[None])
    totals = lax.psum(jnp.stack(packs), WEIGHT_AXES)
    own, other = finish(totals[0], totals[1])
    total = own + other
    sizes = [CONVK * CH, CH, D, DI, H, H, H]
    parts, start = [], 0
    for size in sizes:
        parts.append(total[start : start + size])
        start += size
    share = lambda a, width: lax.dynamic_slice_in_dim(a, share_idx * width, width, axis=a.ndim - 1)
    return (
        act_out,
        grad_out,
        sums[0],
        sums[1],
        share(parts[0].reshape(CONVK, CH), c_loc)[None],
        share(parts[1], c_loc)[None],
        share(parts[2], n_loc)[None],
        share(parts[3], g_loc)[None],
        parts[4][None],
        parts[5][None],
        parts[6][None],
    )


def solution(mesh):
    in_specs = (
        P(None, "dp", "seq", None),
        P(None, "dp", "seq", None),
        P("section", ("dp", "seq"), None),
        P("section", ("dp", "seq"), None),
        P("section", None, ("dp", "seq")),
        P("section", ("dp", "seq")),
        P("section", ("dp", "seq")),
        P("section", ("dp", "seq")),
        P("section", None),
        P("section", None),
        P("section", None),
    )
    out_specs = (
        P("section", None, "dp", "seq", None),
        P("section", None, "dp", "seq", None),
        P("section", ("dp", "seq"), None),
        P("section", ("dp", "seq"), None),
        P("section", None, ("dp", "seq")),
        P("section", ("dp", "seq")),
        P("section", ("dp", "seq")),
        P("section", ("dp", "seq")),
        P("section", None),
        P("section", None),
        P("section", None),
    )
    return jax.shard_map(body, mesh=mesh, in_specs=in_specs, out_specs=out_specs, check_vma=False)
```

```python
import jax
import jax.numpy as jnp
from jax import lax
from jax.experimental import pallas as pl
from jax.experimental.pallas import tpu as pltpu
from jax.sharding import PartitionSpec as P

D = 768
DI = 1536
P_SIZE = 64
N = 128
CONVK = 4
MB = 2
H = 24
CH = 1792
E = 3352
PAIRS = H // 2
PAIR = 2 * P_SIZE
EDGE = 16

EPSILON = 1e-05
PRECISE = lax.Precision.HIGHEST
f32 = jnp.float32
bf16 = jnp.bfloat16
WEIGHT_AXES = ("dp", "seq")


def dot(left, right, dims=((1,), (0,)), precision=None):
    return lax.dot_general(left, right, (dims, ((), ())), preferred_element_type=f32, precision=precision)


def rows_dot(left, right, precision=None):
    return dot(left, right, ((0,), (0,)), precision)


def cols_dot(left, right, precision=None):
    return dot(left, right, ((1,), (1,)), precision)


def shifted(x, axis, by):
    length = lax.axis_size(axis)
    pairs = [(i, i + by) for i in range(length) if 0 <= i + by < length]
    return lax.ppermute(x, axis, pairs)


def swapped(x):
    return lax.ppermute(x, "section", [(0, 1), (1, 0)])


def head_matrix():
    rows = lax.broadcasted_iota(jnp.int32, (H, DI), 0)
    cols = lax.broadcasted_iota(jnp.int32, (H, DI), 1)
    return (rows == cols // P_SIZE).astype(f32)


def expand(values):
    return dot(values, head_matrix(), precision=PRECISE)


def head_sums(values):
    return cols_dot(values, head_matrix(), precision=PRECISE)


def silu_slope(values):
    sigma = jax.nn.sigmoid(values)
    return sigma * (1.0 + values * (1.0 - sigma))


def tied(*values):
    return lax.optimization_barrier(values)


class Halving:
    def __init__(self, grad, late_dp, wire=bf16):
        sizes = {a: lax.axis_size(a) for a in WEIGHT_AXES}
        self.bits = [(a, b) for a in WEIGHT_AXES for b in reversed(range(sizes[a].bit_length() - 1))]
        count = sizes["dp"] * sizes["seq"]
        self.value = grad.astype(wire).reshape(count, grad.shape[0] // count, grad.shape[1])
        dp = sorted(b for b in self.bits if b[0] == "dp")
        seq = sorted(b for b in self.bits if b[0] == "seq")
        self.order = dp[:1] + (seq + dp[1:] if late_dp else dp[1:] + seq)
        self.wire = wire

    def done(self):
        return not self.order

    def step(self):
        if self.done():
            return
        axis, bit = self.order.pop(0)
        place = self.bits.index((axis, bit))
        del self.bits[place]
        rows, cols = self.value.shape[1:]
        halves = self.value.reshape(2**place, 2, 2 ** (len(self.bits) - place), rows, cols)
        upper = (lax.axis_index(axis) >> bit) & 1 == 1
        low, high = halves[:, 0], halves[:, 1]
        keep = jnp.where(upper, high, low)
        pairs = [(i, i ^ (1 << bit)) for i in range(lax.axis_size(axis))]
        got = lax.ppermute(jnp.where(upper, low, high), axis, pairs)
        total = keep.astype(f32) + got.astype(f32)
        if self.bits:
            total = total.astype(self.wire)
        self.value = total.reshape(2 ** len(self.bits), rows, cols)


class Queue:
    def __init__(self):
        self.streams = []

    def add(self, grad, late_dp, wire=bf16):
        stream = Halving(grad, late_dp, wire)
        self.streams.append(stream)
        return stream

    def advance(self, *main):
        live = [s for s in self.streams if not s.done()]
        out = lax.optimization_barrier((main, tuple(s.value for s in live)))
        for stream, value in zip(live, out[1]):
            stream.value = value
            stream.step()
        return out[0] if len(main) > 1 else out[0][0]

    def finish(self):
        while any(not s.done() for s in self.streams):
            for s in self.streams:
                s.step()


def lower_half(shape):
    return lax.broadcasted_iota(jnp.int32, shape, 1) < P_SIZE


def causal_decay(col, row):
    rows = col.shape[0]
    mask = lax.broadcasted_iota(jnp.int32, (rows, rows), 0) >= lax.broadcasted_iota(
        jnp.int32, (rows, rows), 1
    )
    return jnp.exp(jnp.where(mask, col - row, -1e30))


def intra_kernel(x_ref, b_ref, c_ref, cum_ref, cumt_ref, dtt_ref, skip_ref, y_ref, cb_ref):
    @pl.when(pl.program_id(0) == 0)
    def _():
        cb_ref[...] = cols_dot(c_ref[...], b_ref[...])

    x = x_ref[...]
    parts = []
    for i in range(2):
        decay = causal_decay(cum_ref[:, i * P_SIZE : i * P_SIZE + 1], cumt_ref[0, i : i + 1, :])
        mix = (cb_ref[...] * decay * dtt_ref[0, i : i + 1, :]).astype(bf16)
        parts.append(dot(mix, x))
    y = jnp.where(lower_half(x.shape), parts[0], parts[1])
    y_ref[...] = y + skip_ref[...] * x.astype(f32)


def inter_kernel(c_ref, cum_ref, held_ref, part_ref, y_ref):
    c = c_ref[...].astype(f32)
    parts = []
    for i in range(2):
        cdec = (c * jnp.exp(cum_ref[:, i * P_SIZE : i * P_SIZE + 1])).astype(bf16)
        parts.append(dot(cdec, held_ref[...]))
    y_ref[...] = part_ref[...] + jnp.where(lower_half(parts[0].shape), parts[0], parts[1])


def held_grad_kernel(c_ref, cum_ref, dy_ref, out_ref):
    c = c_ref[...].astype(f32)
    parts = []
    for i in range(2):
        cdec = (c * jnp.exp(cum_ref[:, i * P_SIZE : i * P_SIZE + 1])).astype(bf16)
        parts.append(rows_dot(cdec, dy_ref[...]))
    out_ref[...] = jnp.where(lower_half(parts[0].shape), parts[0], parts[1])


def mix_grad_kernel(
    dy_ref,
    x_ref,
    b_ref,
    c_ref,
    cum_ref,
    cumt_ref,
    dtt_ref,
    held_ref,
    skip_ref,
    dx_ref,
    dstep_ref,
    dcum_ref,
    db_ref,
    dc_ref,
    cb_ref,
    dcb_ref,
):
    step = pl.program_id(0)

    @pl.when(step == 0)
    def _():
        cb_ref[...] = cols_dot(c_ref[...], b_ref[...])
        dcb_ref[...] = jnp.zeros_like(dcb_ref)
        dc_ref[...] = jnp.zeros_like(dc_ref)
        dcum_ref[...] = jnp.zeros_like(dcum_ref)

    dy = dy_ref[...]
    x = x_ref[...]
    c = c_ref[...].astype(f32)
    low = lower_half(dy.shape)
    lane = lax.broadcasted_iota(jnp.int32, dcum_ref.shape, 1)
    dx_parts = []
    for i in range(2):
        cum_col = cum_ref[:, i * P_SIZE : i * P_SIZE + 1]
        dt_row = dtt_ref[0, i : i + 1, :]
        decay = causal_decay(cum_col, cumt_ref[0, i : i + 1, :])
        cb_decay = cb_ref[...] * decay
        mix = (cb_decay * dt_row).astype(bf16)
        dx_parts.append(rows_dot(mix, dy))
        own = jnp.where(low if i == 0 else jnp.logical_not(low), dy, jnp.zeros_like(dy))
        dmix = cols_dot(own, x)
        dcb_ref[...] += dmix * decay * dt_row
        inner = dmix * cb_decay
        dstep_ref[0, i : i + 1, :] = jnp.sum(inner, axis=0, keepdims=True)
        grow = jnp.sum(inner * dt_row, axis=1, keepdims=True)
        dcdec = cols_dot(own, held_ref[...])
        grown = dcdec * jnp.exp(cum_col)
        dc_ref[...] += grown
        grow = grow + jnp.sum(grown * c, axis=1, keepdims=True)
        dcum_ref[...] += jnp.where(lane == 2 * step + i, grow, 0.0)
    dx_ref[...] = jnp.where(low, dx_parts[0], dx_parts[1]) + skip_ref[...] * dy.astype(f32)

    @pl.when(step == PAIRS - 1)
    def _():
        dc_ref[...] += dot(dcb_ref[...], b_ref[...].astype(f32), precision=PRECISE)
        db_ref[...] = rows_dot(dcb_ref[...], c, precision=PRECISE)


def by_pair(rows):
    return pl.BlockSpec((rows, PAIR), lambda j: (0, j))


def fixed(rows, block):
    return pl.BlockSpec((rows, PAIR), lambda j: (0, block))


def head_rows(rows):
    return pl.BlockSpec((1, 2, rows), lambda j: (j, 0, 0))


def call(kernel, out_shape, in_specs, out_specs, scratch=()):
    return pl.pallas_call(
        kernel,
        grid=(PAIRS,),
        out_shape=out_shape,
        in_specs=in_specs,
        out_specs=out_specs,
        scratch_shapes=list(scratch),
        compiler_params=pltpu.CompilerParams(vmem_limit_bytes=32 * 1024 * 1024),
    )


def shaped(*shape, dtype=f32):
    return jax.ShapeDtypeStruct(shape, dtype)


B_BLOCK = DI // PAIR
C_BLOCK = B_BLOCK + 1


def intra(acts, cum_wide, cum_t, dt_t, skip_wide):
    t = acts.shape[0]
    return call(
        intra_kernel,
        shaped(t, DI),
        [by_pair(t), fixed(t, B_BLOCK), fixed(t, C_BLOCK), by_pair(t), head_rows(t), head_rows(t), by_pair(1)],
        by_pair(t),
        [pltpu.VMEM((t, t), f32)],
    )(acts, acts, acts, cum_wide, cum_t, dt_t, skip_wide)


def inter(acts, cum_wide, held, part):
    t = acts.shape[0]
    return call(
        inter_kernel,
        shaped(t, DI),
        [fixed(t, C_BLOCK), by_pair(t), by_pair(N), by_pair(t)],
        by_pair(t),
    )(acts, cum_wide, held, part)


def held_grad(acts, cum_wide, dy):
    t = acts.shape[0]
    return call(
        held_grad_kernel,
        shaped(N, DI),
        [fixed(t, C_BLOCK), by_pair(t), by_pair(t)],
        by_pair(N),
    )(acts, cum_wide, dy)


def mix_grad(dy, acts, cum_wide, cum_t, dt_t, held, skip_wide):
    t = acts.shape[0]
    return call(
        mix_grad_kernel,
        (shaped(t, DI), shaped(PAIRS, 2, t), shaped(t, PAIR), shaped(t, N), shaped(t, N)),
        [
            by_pair(t),
            by_pair(t),
            fixed(t, B_BLOCK),
            fixed(t, C_BLOCK),
            by_pair(t),
            head_rows(t),
            head_rows(t),
            by_pair(N),
            by_pair(1),
        ],
        (by_pair(t), head_rows(t), fixed(t, 0), fixed(t, 0), fixed(t, 0)),
        [pltpu.VMEM((t, t), f32), pltpu.VMEM((t, t), f32)],
    )(dy, acts, acts, acts, cum_wide, cum_t, dt_t, held, skip_wide)


def lower_triangle(rows):
    return (
        lax.broadcasted_iota(jnp.int32, (rows, rows), 0)
        >= lax.broadcasted_iota(jnp.int32, (rows, rows), 1)
    ).astype(f32)


def rms_parts(values):
    inv_rms = lax.rsqrt(jnp.mean(values * values, axis=-1, keepdims=True) + EPSILON)
    return inv_rms, values * inv_rms


def layer_forward(layer_in, weights):
    w_in, w_out, conv_w, conv_b, norm_g, gate_g, bias_dt, log_rate, skip_gain = weights
    t = layer_in.shape[0]
    _, normed = rms_parts(layer_in.astype(f32))
    projected = dot((normed * norm_g).astype(bf16), w_in).astype(bf16)
    xbc = projected[:, DI : DI + CH]
    edge = shifted(xbc[t - EDGE :], "seq", 1)
    padded = jnp.concatenate([edge[EDGE - CONVK + 1 :], xbc], axis=0)
    conv = conv_b
    for k in range(CONVK):
        conv = conv + conv_w[k : k + 1] * padded[k : k + t].astype(f32)
    acts = jax.nn.silu(conv).astype(bf16)
    dt = jax.nn.softplus(projected[:, DI + CH : E].astype(f32) + bias_dt)
    cum = dot(lower_triangle(t), dt * -jnp.exp(log_rate), precision=PRECISE)
    to_end = jnp.exp(cum[-1:] - cum)
    factor_wide = expand(dt * to_end)
    weighted = (acts[:, :DI].astype(f32) * factor_wide).astype(bf16)
    states = rows_dot(acts[:, DI : DI + N], weighted)
    totals = jnp.exp(cum[-1:])
    totals_wide = expand(totals)
    incoming = shifted(states.astype(bf16), "seq", 1)
    cum_wide = expand(cum)
    cum_t = cum.T.reshape(PAIRS, 2, t)
    dt_t = dt.T.reshape(PAIRS, 2, t)
    skip_wide = expand(skip_gain)
    part = intra(acts, cum_wide, cum_t, dt_t, skip_wide)
    incoming, part = tied(incoming, part)
    for _ in range(lax.axis_size("seq") - 2):
        incoming = shifted((totals_wide * incoming.astype(f32) + states).astype(bf16), "seq", 1)
    y = inter(acts, cum_wide, incoming, part)
    gate_cols = projected[:, :DI].astype(f32)
    _, q = rms_parts(y * jax.nn.silu(gate_cols))
    mixed = layer_in.astype(f32) + dot((q * gate_g).astype(bf16), w_out)
    kept = (layer_in, projected, padded, acts, conv, dt, cum, cum_wide, cum_t, dt_t, skip_wide, incoming, y, weighted, factor_wide, totals, totals_wide)
    return mixed.astype(bf16), kept


def layer_backward(grad_v, kept, weights, queue):
    w_in, w_out, conv_w, conv_b, norm_g, gate_g, bias_dt, log_rate, skip_gain = weights
    (layer_in, projected, padded, acts, conv, dt, cum, cum_wide, cum_t, dt_t, skip_wide, incoming, y, weighted, factor_wide, totals, totals_wide) = kept
    t = layer_in.shape[0]
    dob = grad_v.astype(bf16)
    z = projected[:, :DI].astype(f32)
    swish = jax.nn.silu(z)
    r2, q = rms_parts(y * swish)
    dyn = cols_dot(dob, w_out)
    grad_gate_gain = jnp.sum(dyn * q, axis=0)
    dq = dyn * gate_g
    dgated = r2 * (dq - q * jnp.mean(dq * q, axis=-1, keepdims=True))
    dz = (dgated * y * silu_slope(z)).astype(bf16)
    dy = (dgated * swish).astype(bf16)
    x = acts[:, :DI].astype(f32)
    grad_skip = head_sums(jnp.sum(dy.astype(f32) * x, axis=0, keepdims=True))[0]
    dheld = held_grad(acts, cum_wide, dy)
    leave = shifted(dheld.astype(bf16), "seq", -1)
    grad_wout = rows_dot((q * gate_g).astype(bf16), dob)
    inv_rms, normed = rms_parts(layer_in.astype(f32))
    un = (normed * norm_g).astype(bf16)
    grad_win_z = rows_dot(un, dz)
    wout_sum = queue.add(grad_wout, False)
    winz_sum = queue.add(grad_win_z, True)
    leave, dy = queue.advance(leave, dy)
    for hop in range(lax.axis_size("seq") - 2):
        leave = shifted((totals_wide * leave.astype(f32) + dheld).astype(bf16), "seq", -1)
        if hop == 0:
            dx, dstep_t, dcum, db, dc = mix_grad(dy, acts, cum_wide, cum_t, dt_t, incoming, skip_wide)
            leave, dx = queue.advance(leave, dx)
    dstep = dstep_t.reshape(H, t).T
    dcum = dcum[:, :H] - dstep * dt
    db = db + cols_dot(weighted, leave)
    dweighted = dot(acts[:, DI : DI + N], leave)
    dx = dx + dweighted * factor_wide
    to_end = jnp.exp(cum[-1:] - cum)
    dfactor = head_sums(dweighted * x)
    dstep = dstep + dfactor * to_end
    dend = dfactor * dt * to_end
    at_total = head_sums(jnp.sum(leave.astype(f32) * incoming.astype(f32), axis=0, keepdims=True))
    last = jnp.sum(dend, axis=0, keepdims=True) + at_total * totals
    is_end = lax.broadcasted_iota(jnp.int32, (t, 1), 0) == t - 1
    dcum = dcum - dend + jnp.where(is_end, last, 0.0)
    drate = rows_dot(lower_triangle(t), dcum, precision=PRECISE)
    rates = -jnp.exp(log_rate)
    dstep = dstep + drate * rates
    grad_alog = jnp.sum(drate * dt, axis=0) * rates[0]
    draw = dstep * jax.nn.sigmoid(projected[:, DI + CH : E].astype(f32) + bias_dt)
    grad_dtb = jnp.sum(draw, axis=0)
    dconv = jnp.concatenate([dx, db, dc], axis=1) * silu_slope(conv)
    edge = shifted(dconv[:8], "seq", -1)
    grad_cb = jnp.sum(dconv, axis=0)
    grad_cw = jnp.stack([jnp.sum(dconv * padded[k : k + t].astype(f32), axis=0) for k in range(CONVK)])
    ext = jnp.concatenate([dconv, edge[: CONVK - 1]], axis=0)
    dxbc = jnp.zeros((t, CH), f32)
    for k in range(CONVK):
        dxbc = dxbc + conv_w[k : k + 1] * ext[CONVK - 1 - k : CONVK - 1 - k + t]
    dxbc = dxbc.astype(bf16)
    draw = draw.astype(bf16)
    half = CH // 2
    winx_sum = queue.add(rows_dot(un, dxbc[:, :half]), False)
    wind_sum = queue.add(rows_dot(un, jnp.concatenate([dxbc[:, half:], draw], axis=1)), True)
    dxbc = queue.advance(dxbc)
    filler = jnp.zeros((t, w_in.shape[1] - E), bf16)
    dun = cols_dot(jnp.concatenate([dz, dxbc, draw, filler], axis=1), w_in)
    grad_norm_gain = jnp.sum(dun * normed, axis=0)
    dnorm = dun * norm_g
    grad_u = grad_v.astype(f32) + inv_rms * (dnorm - normed * jnp.mean(dnorm * normed, axis=-1, keepdims=True))
    count = lax.axis_size("dp") * lax.axis_size("seq")
    heads = jnp.concatenate([grad_dtb, grad_alog, grad_skip])
    rest = jnp.concatenate(
        [
            grad_cw.reshape(CONVK, count, -1).transpose(1, 0, 2).reshape(count, -1),
            grad_cb.reshape(count, -1),
            grad_norm_gain.reshape(count, -1),
            grad_gate_gain.reshape(count, -1),
            jnp.broadcast_to(heads[None], (count, 3 * H)),
        ],
        axis=1,
    )
    rest_sum = queue.add(rest, False, f32)
    return grad_u, (wout_sum, winz_sum, winx_sum, wind_sum, rest_sum)


def body(tokens, cotangent, in_weight, out_weight, conv_weight, conv_bias, norm_gain, gate_gain, dt_bias, a_log, d_skip):
    first = lax.axis_index("section") == 0
    share_count = lax.axis_size("dp") * lax.axis_size("seq")

    def pick(a, b):
        return jnp.where(first, a, b)

    small = jnp.concatenate([conv_weight[0].reshape(-1), conv_bias[0], norm_gain[0], gate_gain[0]])
    rows = in_weight.shape[1]
    extra = -E % 128
    small_count = small.shape[0]
    while rows * extra < small_count:
        extra += 128
    small = jnp.pad(small, (0, rows * extra - small_count)).reshape(rows, extra)
    mine = (jnp.concatenate([in_weight[0], small], axis=1), out_weight[0])
    theirs = tuple(swapped(w) for w in mine)
    heads = jnp.stack([dt_bias[0], a_log[0], d_skip[0]])
    other_heads = swapped(heads)
    head_params = (pick(heads, other_heads), pick(other_heads, heads))
    c_loc, n_loc, g_loc = conv_bias.shape[1], norm_gain.shape[1], gate_gain.shape[1]
    weights = []
    for layer in range(2):
        shards = tuple(pick(m, o) if layer == 0 else pick(o, m) for m, o in zip(mine, theirs))
        w_in, w_out = (lax.all_gather(s, WEIGHT_AXES, axis=0, tiled=True) for s in shards)
        own = w_in[:, E:].reshape(share_count, rows * extra)[:, :small_count].astype(f32)
        cuts = [0, CONVK * c_loc, CONVK * c_loc + c_loc, CONVK * c_loc + c_loc + n_loc]
        conv_w = own[:, : cuts[1]].reshape(share_count, CONVK, c_loc).transpose(1, 0, 2).reshape(CONVK, CH)
        conv_b = own[:, cuts[1] : cuts[2]].reshape(1, CH)
        norm_g = own[:, cuts[2] : cuts[3]].reshape(1, D)
        gate_g = own[:, cuts[3] :].reshape(1, DI)
        hp = head_params[layer]
        weights.append((w_in, w_out, conv_w, conv_b, norm_g, gate_g, hp[0:1], hp[1:2], hp[2:3]))

    stream = pick(tokens[0, 0], tokens[1, 0])
    acts, kept = [], []
    for layer in range(2):
        stream, saved = layer_forward(stream, weights[layer])
        acts.append(stream)
        kept.append(saved)
    grad = pick(cotangent[0, 0], cotangent[1, 0])
    grads, sums = [None, None], [None, None]
    queue = Queue()
    for layer in (1, 0):
        grad, sums[layer] = layer_backward(grad, kept[layer], weights[layer], queue)
        grads[layer] = grad
        grad = grad.astype(bf16)
        if layer == 1:
            grad = queue.advance(grad)
    queue.finish()

    def finish(low, high):
        own = pick(low, high)
        return own, swapped(pick(high, low))

    def by_micro(low, high):
        own, other = finish(low, high)
        return jnp.stack([pick(own, other), pick(other, own)])[None, :, None]

    act_out = by_micro(*acts)
    grad_out = by_micro(*grads)
    shares = []
    for low, high in zip(*sums):
        own = pick(low.value[0], high.value[0])
        other = swapped(pick(high.value[0], low.value[0]).astype(low.wire))
        shares.append(own + other.astype(f32))
    wout, winz, winx, wind, rest = shares
    rest = rest[0]
    parts, start = [], 0
    for size in [CONVK * c_loc, c_loc, n_loc, g_loc, H, H, H]:
        parts.append(rest[start : start + size])
        start += size
    return (
        act_out,
        grad_out,
        jnp.concatenate([winz, winx, wind], axis=1)[None],
        wout[None],
        parts[0].reshape(CONVK, c_loc)[None],
        parts[1][None],
        parts[2][None],
        parts[3][None],
        parts[4][None],
        parts[5][None],
        parts[6][None],
    )


def solution(mesh):
    in_specs = (
        P(None, "dp", "seq", None),
        P(None, "dp", "seq", None),
        P("section", ("dp", "seq"), None),
        P("section", ("dp", "seq"), None),
        P("section", None, ("dp", "seq")),
        P("section", ("dp", "seq")),
        P("section", ("dp", "seq")),
        P("section", ("dp", "seq")),
        P("section", None),
        P("section", None),
        P("section", None),
    )
    out_specs = (
        P("section", None, "dp", "seq", None),
        P("section", None, "dp", "seq", None),
        P("section", ("dp", "seq"), None),
        P("section", ("dp", "seq"), None),
        P("section", None, ("dp", "seq")),
        P("section", ("dp", "seq")),
        P("section", ("dp", "seq")),
        P("section", ("dp", "seq")),
        P("section", None),
        P("section", None),
        P("section", None),
    )
    return jax.shard_map(body, mesh=mesh, in_specs=in_specs, out_specs=out_specs, check_vma=False)
```

```python
import jax
import jax.numpy as jnp
from jax import lax
from jax.experimental import pallas as pl
from jax.experimental.pallas import tpu as pltpu
from jax.sharding import PartitionSpec as P

D = 768
DI = 1536
P_SIZE = 64
N = 128
CONVK = 4
MB = 2
H = 24
CH = 1792
E = 3352
PAIRS = H // 2
PAIR = 2 * P_SIZE
EDGE = 16

EPSILON = 1e-05
PRECISE = lax.Precision.HIGHEST
f32 = jnp.float32
bf16 = jnp.bfloat16
WEIGHT_AXES = ("dp", "seq")


def dot(left, right, dims=((1,), (0,)), precision=None):
    return lax.dot_general(left, right, (dims, ((), ())), preferred_element_type=f32, precision=precision)


def rows_dot(left, right, precision=None):
    return dot(left, right, ((0,), (0,)), precision)


def cols_dot(left, right, precision=None):
    return dot(left, right, ((1,), (1,)), precision)


def shifted(x, axis, by):
    length = lax.axis_size(axis)
    pairs = [(i, i + by) for i in range(length) if 0 <= i + by < length]
    return lax.ppermute(x, axis, pairs)


def swapped(x):
    return lax.ppermute(x, "section", [(0, 1), (1, 0)])


def head_matrix():
    rows = lax.broadcasted_iota(jnp.int32, (H, DI), 0)
    cols = lax.broadcasted_iota(jnp.int32, (H, DI), 1)
    return (rows == cols // P_SIZE).astype(f32)


def expand(values):
    return dot(values, head_matrix(), precision=PRECISE)


def head_sums(values):
    return cols_dot(values, head_matrix(), precision=PRECISE)


def silu_slope(values):
    sigma = jax.nn.sigmoid(values)
    return sigma * (1.0 + values * (1.0 - sigma))


def tied(*values):
    return lax.optimization_barrier(values)


class Halving:
    def __init__(self, grad, late_dp, wire=bf16):
        sizes = {a: lax.axis_size(a) for a in WEIGHT_AXES}
        self.bits = [(a, b) for a in WEIGHT_AXES for b in reversed(range(sizes[a].bit_length() - 1))]
        self.value = grad.astype(wire)
        dp = sorted(b for b in self.bits if b[0] == "dp")
        seq = sorted(b for b in self.bits if b[0] == "seq")
        self.order = dp[:1] + (seq + dp[1:] if late_dp else dp[1:] + seq)
        self.wire = wire

    def done(self):
        return not self.order

    def step(self):
        if self.done():
            return
        axis, bit = self.order.pop(0)
        place = self.bits.index((axis, bit))
        del self.bits[place]
        rows, cols = self.value.shape[1:]
        halves = self.value.reshape(2**place, 2, 2 ** (len(self.bits) - place), rows, cols)
        upper = (lax.axis_index(axis) >> bit) & 1 == 1
        low, high = halves[:, 0], halves[:, 1]
        keep = jnp.where(upper, high, low)
        pairs = [(i, i ^ (1 << bit)) for i in range(lax.axis_size(axis))]
        got = lax.ppermute(jnp.where(upper, low, high), axis, pairs)
        total = keep.astype(f32) + got.astype(f32)
        if self.bits:
            total = total.astype(self.wire)
        self.value = total.reshape(2 ** len(self.bits), rows, cols)


class Queue:
    def __init__(self):
        self.streams = []

    def add(self, grad, late_dp, wire=bf16):
        stream = Halving(grad, late_dp, wire)
        self.streams.append(stream)
        return stream

    def advance(self, *main):
        live = [s for s in self.streams if not s.done()]
        out = lax.optimization_barrier((main, tuple(s.value for s in live)))
        for stream, value in zip(live, out[1]):
            stream.value = value
            stream.step()
        return out[0] if len(main) > 1 else out[0][0]

    def finish(self):
        while any(not s.done() for s in self.streams):
            for s in self.streams:
                s.step()


def lower_half(shape):
    return lax.broadcasted_iota(jnp.int32, shape, 1) < P_SIZE


def causal_decay(col, row):
    rows = col.shape[0]
    mask = lax.broadcasted_iota(jnp.int32, (rows, rows), 0) >= lax.broadcasted_iota(
        jnp.int32, (rows, rows), 1
    )
    return jnp.exp(jnp.where(mask, col - row, -1e30))


def intra_kernel(x_ref, b_ref, c_ref, cum_ref, cumt_ref, dtt_ref, skip_ref, y_ref, cb_ref):
    @pl.when(pl.program_id(0) == 0)
    def _():
        cb_ref[...] = cols_dot(c_ref[...], b_ref[...])

    x = x_ref[...]
    parts = []
    for i in range(2):
        decay = causal_decay(cum_ref[:, i * P_SIZE : i * P_SIZE + 1], cumt_ref[0, i : i + 1, :])
        mix = (cb_ref[...] * decay * dtt_ref[0, i : i + 1, :]).astype(bf16)
        parts.append(dot(mix, x))
    y = jnp.where(lower_half(x.shape), parts[0], parts[1])
    y_ref[...] = y + skip_ref[...] * x.astype(f32)


def inter_kernel(c_ref, cum_ref, held_ref, part_ref, y_ref):
    c = c_ref[...].astype(f32)
    parts = []
    for i in range(2):
        cdec = (c * jnp.exp(cum_ref[:, i * P_SIZE : i * P_SIZE + 1])).astype(bf16)
        parts.append(dot(cdec, held_ref[...]))
    y_ref[...] = part_ref[...] + jnp.where(lower_half(parts[0].shape), parts[0], parts[1])


def held_grad_kernel(c_ref, cum_ref, dy_ref, out_ref):
    c = c_ref[...].astype(f32)
    parts = []
    for i in range(2):
        cdec = (c * jnp.exp(cum_ref[:, i * P_SIZE : i * P_SIZE + 1])).astype(bf16)
        parts.append(rows_dot(cdec, dy_ref[...]))
    out_ref[...] = jnp.where(lower_half(parts[0].shape), parts[0], parts[1])


def mix_grad_kernel(
    dy_ref,
    x_ref,
    b_ref,
    c_ref,
    cum_ref,
    cumt_ref,
    dtt_ref,
    held_ref,
    skip_ref,
    dx_ref,
    dstep_ref,
    dcum_ref,
    db_ref,
    dc_ref,
    cb_ref,
    dcb_ref,
):
    step = pl.program_id(0)

    @pl.when(step == 0)
    def _():
        cb_ref[...] = cols_dot(c_ref[...], b_ref[...])
        dcb_ref[...] = jnp.zeros_like(dcb_ref)
        dc_ref[...] = jnp.zeros_like(dc_ref)
        dcum_ref[...] = jnp.zeros_like(dcum_ref)

    dy = dy_ref[...]
    x = x_ref[...]
    c = c_ref[...].astype(f32)
    low = lower_half(dy.shape)
    lane = lax.broadcasted_iota(jnp.int32, dcum_ref.shape, 1)
    dx_parts = []
    for i in range(2):
        cum_col = cum_ref[:, i * P_SIZE : i * P_SIZE + 1]
        dt_row = dtt_ref[0, i : i + 1, :]
        decay = causal_decay(cum_col, cumt_ref[0, i : i + 1, :])
        cb_decay = cb_ref[...] * decay
        mix = (cb_decay * dt_row).astype(bf16)
        dx_parts.append(rows_dot(mix, dy))
        own = jnp.where(low if i == 0 else jnp.logical_not(low), dy, jnp.zeros_like(dy))
        dmix = cols_dot(own, x)
        dcb_ref[...] += dmix * decay * dt_row
        inner = dmix * cb_decay
        dstep_ref[0, i : i + 1, :] = jnp.sum(inner, axis=0, keepdims=True)
        grow = jnp.sum(inner * dt_row, axis=1, keepdims=True)
        dcdec = cols_dot(own, held_ref[...])
        grown = dcdec * jnp.exp(cum_col)
        dc_ref[...] += grown
        grow = grow + jnp.sum(grown * c, axis=1, keepdims=True)
        dcum_ref[...] += jnp.where(lane == 2 * step + i, grow, 0.0)
    dx_ref[...] = jnp.where(low, dx_parts[0], dx_parts[1]) + skip_ref[...] * dy.astype(f32)

    @pl.when(step == PAIRS - 1)
    def _():
        dc_ref[...] += dot(dcb_ref[...], b_ref[...].astype(f32), precision=PRECISE)
        db_ref[...] = rows_dot(dcb_ref[...], c, precision=PRECISE)


def by_pair(rows):
    return pl.BlockSpec((rows, PAIR), lambda j: (0, j))


def fixed(rows, block):
    return pl.BlockSpec((rows, PAIR), lambda j: (0, block))


def head_rows(rows):
    return pl.BlockSpec((1, 2, rows), lambda j: (j, 0, 0))


def call(kernel, out_shape, in_specs, out_specs, scratch=()):
    return pl.pallas_call(
        kernel,
        grid=(PAIRS,),
        out_shape=out_shape,
        in_specs=in_specs,
        out_specs=out_specs,
        scratch_shapes=list(scratch),
        compiler_params=pltpu.CompilerParams(vmem_limit_bytes=32 * 1024 * 1024),
    )


def shaped(*shape, dtype=f32):
    return jax.ShapeDtypeStruct(shape, dtype)


B_BLOCK = DI // PAIR
C_BLOCK = B_BLOCK + 1


def intra(acts, cum_wide, cum_t, dt_t, skip_wide):
    t = acts.shape[0]
    return call(
        intra_kernel,
        shaped(t, DI),
        [by_pair(t), fixed(t, B_BLOCK), fixed(t, C_BLOCK), by_pair(t), head_rows(t), head_rows(t), by_pair(1)],
        by_pair(t),
        [pltpu.VMEM((t, t), f32)],
    )(acts, acts, acts, cum_wide, cum_t, dt_t, skip_wide)


def inter(acts, cum_wide, held, part):
    t = acts.shape[0]
    return call(
        inter_kernel,
        shaped(t, DI),
        [fixed(t, C_BLOCK), by_pair(t), by_pair(N), by_pair(t)],
        by_pair(t),
    )(acts, cum_wide, held, part)


def held_grad(acts, cum_wide, dy):
    t = acts.shape[0]
    return call(
        held_grad_kernel,
        shaped(N, DI),
        [fixed(t, C_BLOCK), by_pair(t), by_pair(t)],
        by_pair(N),
    )(acts, cum_wide, dy)


def mix_grad(dy, acts, cum_wide, cum_t, dt_t, held, skip_wide):
    t = acts.shape[0]
    return call(
        mix_grad_kernel,
        (shaped(t, DI), shaped(PAIRS, 2, t), shaped(t, PAIR), shaped(t, N), shaped(t, N)),
        [
            by_pair(t),
            by_pair(t),
            fixed(t, B_BLOCK),
            fixed(t, C_BLOCK),
            by_pair(t),
            head_rows(t),
            head_rows(t),
            by_pair(N),
            by_pair(1),
        ],
        (by_pair(t), head_rows(t), fixed(t, 0), fixed(t, 0), fixed(t, 0)),
        [pltpu.VMEM((t, t), f32), pltpu.VMEM((t, t), f32)],
    )(dy, acts, acts, acts, cum_wide, cum_t, dt_t, held, skip_wide)


def lower_triangle(rows):
    return (
        lax.broadcasted_iota(jnp.int32, (rows, rows), 0)
        >= lax.broadcasted_iota(jnp.int32, (rows, rows), 1)
    ).astype(f32)


def rms_parts(values):
    inv_rms = lax.rsqrt(jnp.mean(values * values, axis=-1, keepdims=True) + EPSILON)
    return inv_rms, values * inv_rms


def layer_forward(layer_in, weights):
    w_in, w_out, conv_w, conv_b, norm_g, gate_g, bias_dt, log_rate, skip_gain = weights
    t = layer_in.shape[0]
    _, normed = rms_parts(layer_in.astype(f32))
    projected = dot((normed * norm_g).astype(bf16), w_in).astype(bf16)
    xbc = projected[:, DI : DI + CH]
    edge = shifted(xbc[t - EDGE :], "seq", 1)
    padded = jnp.concatenate([edge[EDGE - CONVK + 1 :], xbc], axis=0)
    conv = conv_b
    for k in range(CONVK):
        conv = conv + conv_w[k : k + 1] * padded[k : k + t].astype(f32)
    acts = jax.nn.silu(conv).astype(bf16)
    dt = jax.nn.softplus(projected[:, DI + CH : E].astype(f32) + bias_dt)
    cum = dot(lower_triangle(t), dt * -jnp.exp(log_rate), precision=PRECISE)
    to_end = jnp.exp(cum[-1:] - cum)
    factor_wide = expand(dt * to_end)
    weighted = (acts[:, :DI].astype(f32) * factor_wide).astype(bf16)
    states = rows_dot(acts[:, DI : DI + N], weighted)
    totals = jnp.exp(cum[-1:])
    totals_wide = expand(totals)
    incoming = shifted(states.astype(bf16), "seq", 1)
    cum_wide = expand(cum)
    cum_t = cum.T.reshape(PAIRS, 2, t)
    dt_t = dt.T.reshape(PAIRS, 2, t)
    skip_wide = expand(skip_gain)
    part = intra(acts, cum_wide, cum_t, dt_t, skip_wide)
    incoming, part = tied(incoming, part)
    for _ in range(lax.axis_size("seq") - 2):
        incoming = shifted((totals_wide * incoming.astype(f32) + states).astype(bf16), "seq", 1)
    y = inter(acts, cum_wide, incoming, part)
    gate_cols = projected[:, :DI].astype(f32)
    _, q = rms_parts(y * jax.nn.silu(gate_cols))
    mixed = layer_in.astype(f32) + dot((q * gate_g).astype(bf16), w_out)
    kept = (layer_in, projected, padded, acts, conv, dt, cum, cum_wide, cum_t, dt_t, skip_wide, incoming, y, weighted, factor_wide, totals, totals_wide)
    return mixed.astype(bf16), kept


def layer_backward(grad_v, kept, weights, queue):
    w_in, w_out, conv_w, conv_b, norm_g, gate_g, bias_dt, log_rate, skip_gain = weights
    (layer_in, projected, padded, acts, conv, dt, cum, cum_wide, cum_t, dt_t, skip_wide, incoming, y, weighted, factor_wide, totals, totals_wide) = kept
    t = layer_in.shape[0]
    dob = grad_v.astype(bf16)
    z = projected[:, :DI].astype(f32)
    swish = jax.nn.silu(z)
    r2, q = rms_parts(y * swish)
    dyn = cols_dot(dob, w_out)
    grad_gate_gain = jnp.sum(dyn * q, axis=0)
    dq = dyn * gate_g
    dgated = r2 * (dq - q * jnp.mean(dq * q, axis=-1, keepdims=True))
    dz = (dgated * y * silu_slope(z)).astype(bf16)
    dy = (dgated * swish).astype(bf16)
    x = acts[:, :DI].astype(f32)
    grad_skip = head_sums(jnp.sum(dy.astype(f32) * x, axis=0, keepdims=True))[0]
    dheld = held_grad(acts, cum_wide, dy)
    leave = shifted(dheld.astype(bf16), "seq", -1)
    grad_wout = rows_dot((q * gate_g).astype(bf16), dob)
    inv_rms, normed = rms_parts(layer_in.astype(f32))
    un = (normed * norm_g).astype(bf16)
    grad_win_z = rows_dot(un, dz)
    count = lax.axis_size("dp") * lax.axis_size("seq")
    early = jnp.concatenate(
        [*grad_wout.astype(bf16).reshape(count, 2, -1, D).transpose(1, 0, 2, 3), grad_win_z.astype(bf16).reshape(count, -1, DI)],
        axis=2,
    )
    early_sum = queue.add(early, False)
    leave, dy = queue.advance(leave, dy)
    for hop in range(lax.axis_size("seq") - 2):
        leave = shifted((totals_wide * leave.astype(f32) + dheld).astype(bf16), "seq", -1)
        if hop == 0:
            dx, dstep_t, dcum, db, dc = mix_grad(dy, acts, cum_wide, cum_t, dt_t, incoming, skip_wide)
            leave, dx = queue.advance(leave, dx)
    leave, dx = queue.advance(leave, dx)
    dstep = dstep_t.reshape(H, t).T
    dcum = dcum[:, :H] - dstep * dt
    db = db + cols_dot(weighted, leave)
    dweighted = dot(acts[:, DI : DI + N], leave)
    dx = dx + dweighted * factor_wide
    to_end = jnp.exp(cum[-1:] - cum)
    dfactor = head_sums(dweighted * x)
    dstep = dstep + dfactor * to_end
    dend = dfactor * dt * to_end
    at_total = head_sums(jnp.sum(leave.astype(f32) * incoming.astype(f32), axis=0, keepdims=True))
    last = jnp.sum(dend, axis=0, keepdims=True) + at_total * totals
    is_end = lax.broadcasted_iota(jnp.int32, (t, 1), 0) == t - 1
    dcum = dcum - dend + jnp.where(is_end, last, 0.0)
    drate = rows_dot(lower_triangle(t), dcum, precision=PRECISE)
    rates = -jnp.exp(log_rate)
    dstep = dstep + drate * rates
    grad_alog = jnp.sum(drate * dt, axis=0) * rates[0]
    draw = dstep * jax.nn.sigmoid(projected[:, DI + CH : E].astype(f32) + bias_dt)
    grad_dtb = jnp.sum(draw, axis=0)
    dconv = jnp.concatenate([dx, db, dc], axis=1) * silu_slope(conv)
    dconv = queue.advance(dconv)
    edge = shifted(dconv[:8], "seq", -1)
    grad_cb = jnp.sum(dconv, axis=0)
    grad_cw = jnp.stack([jnp.sum(dconv * padded[k : k + t].astype(f32), axis=0) for k in range(CONVK)])
    ext = jnp.concatenate([dconv, edge[: CONVK - 1]], axis=0)
    dxbc = jnp.zeros((t, CH), f32)
    for k in range(CONVK):
        dxbc = dxbc + conv_w[k : k + 1] * ext[CONVK - 1 - k : CONVK - 1 - k + t]
    dxbc = dxbc.astype(bf16)
    draw = draw.astype(bf16)
    late = rows_dot(un, jnp.concatenate([dxbc, draw], axis=1)).astype(bf16)
    late_sum = queue.add(late.reshape(count, -1, CH + H), False)
    dxbc = queue.advance(dxbc)
    filler = jnp.zeros((t, w_in.shape[1] - E), bf16)
    dun = cols_dot(jnp.concatenate([dz, dxbc, draw, filler], axis=1), w_in)
    grad_norm_gain = jnp.sum(dun * normed, axis=0)
    dnorm = dun * norm_g
    grad_u = grad_v.astype(f32) + inv_rms * (dnorm - normed * jnp.mean(dnorm * normed, axis=-1, keepdims=True))
    rest = (grad_cw, grad_cb, grad_norm_gain, grad_gate_gain, grad_dtb, grad_alog, grad_skip)
    rest = lax.psum(jnp.concatenate([r.reshape(-1) for r in rest]), ("section",) + WEIGHT_AXES)
    return grad_u, (early_sum, late_sum), rest


def body(tokens, cotangent, in_weight, out_weight, conv_weight, conv_bias, norm_gain, gate_gain, dt_bias, a_log, d_skip):
    first = lax.axis_index("section") == 0
    share_count = lax.axis_size("dp") * lax.axis_size("seq")

    def pick(a, b):
        return jnp.where(first, a, b)

    small = jnp.concatenate([conv_weight[0].reshape(-1), conv_bias[0], norm_gain[0], gate_gain[0]])
    rows = in_weight.shape[1]
    extra = -E % 128
    small_count = small.shape[0]
    while rows * extra < small_count:
        extra += 128
    small = jnp.pad(small, (0, rows * extra - small_count)).reshape(rows, extra)
    mine = (jnp.concatenate([in_weight[0], small], axis=1), out_weight[0])
    theirs = tuple(swapped(w) for w in mine)
    heads = jnp.stack([dt_bias[0], a_log[0], d_skip[0]])
    other_heads = swapped(heads)
    head_params = (pick(heads, other_heads), pick(other_heads, heads))
    c_loc, n_loc, g_loc = conv_bias.shape[1], norm_gain.shape[1], gate_gain.shape[1]
    gathered = []
    for layer in range(2):
        shards = tuple(pick(m, o) if layer == 0 else pick(o, m) for m, o in zip(mine, theirs))
        gathered.append(tuple(lax.all_gather(s, WEIGHT_AXES, axis=0, tiled=True) for s in shards))

    def unpacked(layer, w_in, w_out):
        own = w_in[:, E:].reshape(share_count, rows * extra)[:, :small_count].astype(f32)
        cuts = [0, CONVK * c_loc, CONVK * c_loc + c_loc, CONVK * c_loc + c_loc + n_loc]
        conv_w = own[:, : cuts[1]].reshape(share_count, CONVK, c_loc).transpose(1, 0, 2).reshape(CONVK, CH)
        conv_b = own[:, cuts[1] : cuts[2]].reshape(1, CH)
        norm_g = own[:, cuts[2] : cuts[3]].reshape(1, D)
        gate_g = own[:, cuts[3] :].reshape(1, DI)
        hp = head_params[layer]
        return (w_in, w_out, conv_w, conv_b, norm_g, gate_g, hp[0:1], hp[1:2], hp[2:3])

    stream = pick(tokens[0, 0], tokens[1, 0])
    acts, kept, weights = [], [], []
    for layer in range(2):
        w_in, w_out = gathered[layer]
        if layer > 0:
            stream, w_in, w_out = tied(stream, w_in, w_out)
        weights.append(unpacked(layer, w_in, w_out))
        stream, saved = layer_forward(stream, weights[layer])
        acts.append(stream)
        kept.append(saved)
    grad = pick(cotangent[0, 0], cotangent[1, 0])
    grads, sums, rests = [None, None], [None, None], [None, None]
    queue = Queue()
    for layer in (1, 0):
        grad, sums[layer], rests[layer] = layer_backward(grad, kept[layer], weights[layer], queue)
        grads[layer] = grad
        grad = grad.astype(bf16)
        if layer == 1:
            grad = queue.advance(grad)
    queue.finish()

    def finish(low, high):
        own = pick(low, high)
        return own, swapped(pick(high, low))

    def by_micro(low, high):
        own, other = finish(low, high)
        return jnp.stack([pick(own, other), pick(other, own)])[None, :, None]

    act_out = by_micro(*acts)
    grad_out = by_micro(*grads)
    shares = []
    for low, high in zip(*sums):
        own = pick(low.value[0], high.value[0])
        other = swapped(pick(high.value[0], low.value[0]).astype(low.wire))
        shares.append(own + other.astype(f32))
    early, late = shares
    wout = jnp.concatenate([early[:, :D], early[:, D : 2 * D]], axis=0)
    rest = pick(*rests)
    parts, start = [], 0
    for size in [CONVK * CH, CH, D, DI, H, H, H]:
        parts.append(rest[start : start + size])
        start += size
    share_idx = lax.axis_index("dp") * lax.axis_size("seq") + lax.axis_index("seq")
    share = lambda a, width: lax.dynamic_slice_in_dim(a, share_idx * width, width, axis=a.ndim - 1)
    return (
        act_out,
        grad_out,
        jnp.concatenate([early[:, 2 * D :], late], axis=1)[None],
        wout[None],
        share(parts[0].reshape(CONVK, CH), c_loc)[None],
        share(parts[1], c_loc)[None],
        share(parts[2], n_loc)[None],
        share(parts[3], g_loc)[None],
        parts[4][None],
        parts[5][None],
        parts[6][None],
    )


def solution(mesh):
    in_specs = (
        P(None, "dp", "seq", None),
        P(None, "dp", "seq", None),
        P("section", ("dp", "seq"), None),
        P("section", ("dp", "seq"), None),
        P("section", None, ("dp", "seq")),
        P("section", ("dp", "seq")),
        P("section", ("dp", "seq")),
        P("section", ("dp", "seq")),
        P("section", None),
        P("section", None),
        P("section", None),
    )
    out_specs = (
        P("section", None, "dp", "seq", None),
        P("section", None, "dp", "seq", None),
        P("section", ("dp", "seq"), None),
        P("section", ("dp", "seq"), None),
        P("section", None, ("dp", "seq")),
        P("section", ("dp", "seq")),
        P("section", ("dp", "seq")),
        P("section", ("dp", "seq")),
        P("section", None),
        P("section", None),
        P("section", None),
    )
    return jax.shard_map(body, mesh=mesh, in_specs=in_specs, out_specs=out_specs, check_vma=False)
```

```python
import jax
import jax.numpy as jnp
from jax import lax
from jax.experimental import pallas as pl
from jax.experimental.pallas import tpu as pltpu
from jax.sharding import PartitionSpec as P

D = 768
DI = 1536
P_SIZE = 64
N = 128
CONVK = 4
MB = 2
H = 24
CH = 1792
E = 3352
PAIRS = H // 2
PAIR = 2 * P_SIZE
EDGE = 16

EPSILON = 1e-05
PRECISE = lax.Precision.HIGHEST
f32 = jnp.float32
bf16 = jnp.bfloat16
WEIGHT_AXES = ("dp", "seq")


def dot(left, right, dims=((1,), (0,)), precision=None):
    return lax.dot_general(left, right, (dims, ((), ())), preferred_element_type=f32, precision=precision)


def rows_dot(left, right, precision=None):
    return dot(left, right, ((0,), (0,)), precision)


def cols_dot(left, right, precision=None):
    return dot(left, right, ((1,), (1,)), precision)


def shifted(x, axis, by):
    length = lax.axis_size(axis)
    pairs = [(i, i + by) for i in range(length) if 0 <= i + by < length]
    return lax.ppermute(x, axis, pairs)


def swapped(x):
    return lax.ppermute(x, "section", [(0, 1), (1, 0)])


def head_matrix():
    rows = lax.broadcasted_iota(jnp.int32, (H, DI), 0)
    cols = lax.broadcasted_iota(jnp.int32, (H, DI), 1)
    return (rows == cols // P_SIZE).astype(f32)


def expand(values):
    return dot(values, head_matrix(), precision=PRECISE)


def head_sums(values):
    return cols_dot(values, head_matrix(), precision=PRECISE)


def silu_slope(values):
    sigma = jax.nn.sigmoid(values)
    return sigma * (1.0 + values * (1.0 - sigma))


def tied(*values):
    return lax.optimization_barrier(values)


class Halving:
    def __init__(self, grad, late_dp, wire=bf16):
        sizes = {a: lax.axis_size(a) for a in WEIGHT_AXES}
        self.bits = [(a, b) for a in WEIGHT_AXES for b in reversed(range(sizes[a].bit_length() - 1))]
        self.value = grad.astype(wire)
        dp = sorted(b for b in self.bits if b[0] == "dp")
        seq = sorted(b for b in self.bits if b[0] == "seq")
        self.order = dp[:1] + (seq + dp[1:] if late_dp else dp[1:] + seq)
        self.wire = wire

    def done(self):
        return not self.order

    def step(self):
        if self.done():
            return
        axis, bit = self.order.pop(0)
        place = self.bits.index((axis, bit))
        del self.bits[place]
        rows, cols = self.value.shape[1:]
        halves = self.value.reshape(2**place, 2, 2 ** (len(self.bits) - place), rows, cols)
        upper = (lax.axis_index(axis) >> bit) & 1 == 1
        low, high = halves[:, 0], halves[:, 1]
        keep = jnp.where(upper, high, low)
        pairs = [(i, i ^ (1 << bit)) for i in range(lax.axis_size(axis))]
        got = lax.ppermute(jnp.where(upper, low, high), axis, pairs)
        total = keep.astype(f32) + got.astype(f32)
        if self.bits:
            total = total.astype(self.wire)
        self.value = total.reshape(2 ** len(self.bits), rows, cols)


class Queue:
    def __init__(self):
        self.streams = []

    def add(self, grad, late_dp, wire=bf16):
        stream = Halving(grad, late_dp, wire)
        self.streams.append(stream)
        return stream

    def advance(self, *main):
        live = [s for s in self.streams if not s.done()]
        out = lax.optimization_barrier((main, tuple(s.value for s in live)))
        for stream, value in zip(live, out[1]):
            stream.value = value
            stream.step()
        return out[0] if len(main) > 1 else out[0][0]

    def finish(self):
        while any(not s.done() for s in self.streams):
            for s in self.streams:
                s.step()


def lower_half(shape):
    return lax.broadcasted_iota(jnp.int32, shape, 1) < P_SIZE


def causal_decay(col, row):
    rows = col.shape[0]
    mask = lax.broadcasted_iota(jnp.int32, (rows, rows), 0) >= lax.broadcasted_iota(
        jnp.int32, (rows, rows), 1
    )
    return jnp.exp(jnp.where(mask, col - row, -1e30))


def intra_kernel(x_ref, b_ref, c_ref, cum_ref, cumt_ref, dtt_ref, skip_ref, y_ref, cb_ref):
    @pl.when(pl.program_id(0) == 0)
    def _():
        cb_ref[...] = cols_dot(c_ref[...], b_ref[...])

    x = x_ref[...]
    parts = []
    for i in range(2):
        decay = causal_decay(cum_ref[:, i * P_SIZE : i * P_SIZE + 1], cumt_ref[0, i : i + 1, :])
        mix = (cb_ref[...] * decay * dtt_ref[0, i : i + 1, :]).astype(bf16)
        parts.append(dot(mix, x))
    y = jnp.where(lower_half(x.shape), parts[0], parts[1])
    y_ref[...] = y + skip_ref[...] * x.astype(f32)


def inter_kernel(c_ref, cum_ref, held_ref, part_ref, y_ref):
    c = c_ref[...].astype(f32)
    parts = []
    for i in range(2):
        cdec = (c * jnp.exp(cum_ref[:, i * P_SIZE : i * P_SIZE + 1])).astype(bf16)
        parts.append(dot(cdec, held_ref[...]))
    y_ref[...] = part_ref[...] + jnp.where(lower_half(parts[0].shape), parts[0], parts[1])


def held_grad_kernel(c_ref, cum_ref, dy_ref, out_ref):
    c = c_ref[...].astype(f32)
    parts = []
    for i in range(2):
        cdec = (c * jnp.exp(cum_ref[:, i * P_SIZE : i * P_SIZE + 1])).astype(bf16)
        parts.append(rows_dot(cdec, dy_ref[...]))
    out_ref[...] = jnp.where(lower_half(parts[0].shape), parts[0], parts[1])


def mix_grad_kernel(
    dy_ref,
    x_ref,
    b_ref,
    c_ref,
    cum_ref,
    cumt_ref,
    dtt_ref,
    held_ref,
    skip_ref,
    dx_ref,
    dstep_ref,
    dcum_ref,
    db_ref,
    dc_ref,
    cb_ref,
    dcb_ref,
):
    step = pl.program_id(0)

    @pl.when(step == 0)
    def _():
        cb_ref[...] = cols_dot(c_ref[...], b_ref[...])
        dcb_ref[...] = jnp.zeros_like(dcb_ref)
        dc_ref[...] = jnp.zeros_like(dc_ref)
        dcum_ref[...] = jnp.zeros_like(dcum_ref)

    dy = dy_ref[...]
    x = x_ref[...]
    c = c_ref[...].astype(f32)
    low = lower_half(dy.shape)
    lane = lax.broadcasted_iota(jnp.int32, dcum_ref.shape, 1)
    dx_parts = []
    for i in range(2):
        cum_col = cum_ref[:, i * P_SIZE : i * P_SIZE + 1]
        dt_row = dtt_ref[0, i : i + 1, :]
        decay = causal_decay(cum_col, cumt_ref[0, i : i + 1, :])
        cb_decay = cb_ref[...] * decay
        mix = (cb_decay * dt_row).astype(bf16)
        dx_parts.append(rows_dot(mix, dy))
        own = jnp.where(low if i == 0 else jnp.logical_not(low), dy, jnp.zeros_like(dy))
        dmix = cols_dot(own, x)
        dcb_ref[...] += dmix * decay * dt_row
        inner = dmix * cb_decay
        dstep_ref[0, i : i + 1, :] = jnp.sum(inner, axis=0, keepdims=True)
        grow = jnp.sum(inner * dt_row, axis=1, keepdims=True)
        dcdec = cols_dot(own, held_ref[...])
        grown = dcdec * jnp.exp(cum_col)
        dc_ref[...] += grown
        grow = grow + jnp.sum(grown * c, axis=1, keepdims=True)
        dcum_ref[...] += jnp.where(lane == 2 * step + i, grow, 0.0)
    dx_ref[...] = jnp.where(low, dx_parts[0], dx_parts[1]) + skip_ref[...] * dy.astype(f32)

    @pl.when(step == PAIRS - 1)
    def _():
        dc_ref[...] += dot(dcb_ref[...], b_ref[...].astype(f32), precision=PRECISE)
        db_ref[...] = rows_dot(dcb_ref[...], c, precision=PRECISE)


def by_pair(rows):
    return pl.BlockSpec((rows, PAIR), lambda j: (0, j))


def fixed(rows, block):
    return pl.BlockSpec((rows, PAIR), lambda j: (0, block))


def head_rows(rows):
    return pl.BlockSpec((1, 2, rows), lambda j: (j, 0, 0))


def call(kernel, out_shape, in_specs, out_specs, scratch=()):
    return pl.pallas_call(
        kernel,
        grid=(PAIRS,),
        out_shape=out_shape,
        in_specs=in_specs,
        out_specs=out_specs,
        scratch_shapes=list(scratch),
        compiler_params=pltpu.CompilerParams(vmem_limit_bytes=32 * 1024 * 1024),
    )


def shaped(*shape, dtype=f32):
    return jax.ShapeDtypeStruct(shape, dtype)


B_BLOCK = DI // PAIR
C_BLOCK = B_BLOCK + 1


def intra(acts, cum_wide, cum_t, dt_t, skip_wide):
    t = acts.shape[0]
    return call(
        intra_kernel,
        shaped(t, DI),
        [by_pair(t), fixed(t, B_BLOCK), fixed(t, C_BLOCK), by_pair(t), head_rows(t), head_rows(t), by_pair(1)],
        by_pair(t),
        [pltpu.VMEM((t, t), f32)],
    )(acts, acts, acts, cum_wide, cum_t, dt_t, skip_wide)


def inter(acts, cum_wide, held, part):
    t = acts.shape[0]
    return call(
        inter_kernel,
        shaped(t, DI),
        [fixed(t, C_BLOCK), by_pair(t), by_pair(N), by_pair(t)],
        by_pair(t),
    )(acts, cum_wide, held, part)


def held_grad(acts, cum_wide, dy):
    t = acts.shape[0]
    return call(
        held_grad_kernel,
        shaped(N, DI),
        [fixed(t, C_BLOCK), by_pair(t), by_pair(t)],
        by_pair(N),
    )(acts, cum_wide, dy)


def mix_grad(dy, acts, cum_wide, cum_t, dt_t, held, skip_wide):
    t = acts.shape[0]
    return call(
        mix_grad_kernel,
        (shaped(t, DI), shaped(PAIRS, 2, t), shaped(t, PAIR), shaped(t, N), shaped(t, N)),
        [
            by_pair(t),
            by_pair(t),
            fixed(t, B_BLOCK),
            fixed(t, C_BLOCK),
            by_pair(t),
            head_rows(t),
            head_rows(t),
            by_pair(N),
            by_pair(1),
        ],
        (by_pair(t), head_rows(t), fixed(t, 0), fixed(t, 0), fixed(t, 0)),
        [pltpu.VMEM((t, t), f32), pltpu.VMEM((t, t), f32)],
    )(dy, acts, acts, acts, cum_wide, cum_t, dt_t, held, skip_wide)


def lower_triangle(rows):
    return (
        lax.broadcasted_iota(jnp.int32, (rows, rows), 0)
        >= lax.broadcasted_iota(jnp.int32, (rows, rows), 1)
    ).astype(f32)


def rms_parts(values):
    inv_rms = lax.rsqrt(jnp.mean(values * values, axis=-1, keepdims=True) + EPSILON)
    return inv_rms, values * inv_rms


def layer_forward(layer_in, weights, awaited=()):
    w_in, w_out, conv_w, conv_b, norm_g, gate_g, bias_dt, log_rate, skip_gain = weights
    t = layer_in.shape[0]
    _, normed = rms_parts(layer_in.astype(f32))
    projected = dot((normed * norm_g).astype(bf16), w_in).astype(bf16)
    xbc = projected[:, DI : DI + CH]
    edge = shifted(xbc[t - EDGE :], "seq", 1)
    padded = jnp.concatenate([edge[EDGE - CONVK + 1 :], xbc], axis=0)
    conv = conv_b
    for k in range(CONVK):
        conv = conv + conv_w[k : k + 1] * padded[k : k + t].astype(f32)
    acts = jax.nn.silu(conv).astype(bf16)
    dt = jax.nn.softplus(projected[:, DI + CH : E].astype(f32) + bias_dt)
    cum = dot(lower_triangle(t), dt * -jnp.exp(log_rate), precision=PRECISE)
    to_end = jnp.exp(cum[-1:] - cum)
    factor_wide = expand(dt * to_end)
    weighted = (acts[:, :DI].astype(f32) * factor_wide).astype(bf16)
    states = rows_dot(acts[:, DI : DI + N], weighted)
    totals = jnp.exp(cum[-1:])
    totals_wide = expand(totals)
    incoming = shifted(states.astype(bf16), "seq", 1)
    cum_wide = expand(cum)
    cum_t = cum.T.reshape(PAIRS, 2, t)
    dt_t = dt.T.reshape(PAIRS, 2, t)
    skip_wide = expand(skip_gain)
    part = intra(acts, cum_wide, cum_t, dt_t, skip_wide)
    incoming, part, *awaited = tied(incoming, part, *awaited)
    for _ in range(lax.axis_size("seq") - 2):
        incoming = shifted((totals_wide * incoming.astype(f32) + states).astype(bf16), "seq", 1)
    y = inter(acts, cum_wide, incoming, part)
    gate_cols = projected[:, :DI].astype(f32)
    _, q = rms_parts(y * jax.nn.silu(gate_cols))
    mixed = layer_in.astype(f32) + dot((q * gate_g).astype(bf16), w_out)
    kept = (layer_in, projected, padded, acts, conv, dt, cum, cum_wide, cum_t, dt_t, skip_wide, incoming, y, weighted, factor_wide, totals, totals_wide)
    return mixed.astype(bf16), kept, awaited


def layer_backward(grad_v, kept, weights, queue):
    w_in, w_out, conv_w, conv_b, norm_g, gate_g, bias_dt, log_rate, skip_gain = weights
    (layer_in, projected, padded, acts, conv, dt, cum, cum_wide, cum_t, dt_t, skip_wide, incoming, y, weighted, factor_wide, totals, totals_wide) = kept
    t = layer_in.shape[0]
    dob = grad_v.astype(bf16)
    z = projected[:, :DI].astype(f32)
    swish = jax.nn.silu(z)
    r2, q = rms_parts(y * swish)
    dyn = cols_dot(dob, w_out)
    grad_gate_gain = jnp.sum(dyn * q, axis=0)
    dq = dyn * gate_g
    dgated = r2 * (dq - q * jnp.mean(dq * q, axis=-1, keepdims=True))
    dz = (dgated * y * silu_slope(z)).astype(bf16)
    dy = (dgated * swish).astype(bf16)
    x = acts[:, :DI].astype(f32)
    grad_skip = head_sums(jnp.sum(dy.astype(f32) * x, axis=0, keepdims=True))[0]
    dheld = held_grad(acts, cum_wide, dy)
    leave = shifted(dheld.astype(bf16), "seq", -1)
    grad_wout = rows_dot((q * gate_g).astype(bf16), dob)
    inv_rms, normed = rms_parts(layer_in.astype(f32))
    un = (normed * norm_g).astype(bf16)
    grad_win_z = rows_dot(un, dz)
    count = lax.axis_size("dp") * lax.axis_size("seq")
    early = jnp.concatenate(
        [*grad_wout.astype(bf16).reshape(count, 2, -1, D).transpose(1, 0, 2, 3), grad_win_z.astype(bf16).reshape(count, -1, DI)],
        axis=2,
    )
    early_sum = queue.add(early, False)
    leave, dy = queue.advance(leave, dy)
    for hop in range(lax.axis_size("seq") - 2):
        leave = shifted((totals_wide * leave.astype(f32) + dheld).astype(bf16), "seq", -1)
        if hop == 0:
            dx, dstep_t, dcum, db, dc = mix_grad(dy, acts, cum_wide, cum_t, dt_t, incoming, skip_wide)
            leave, dx = queue.advance(leave, dx)
    leave, dx = queue.advance(leave, dx)
    dstep = dstep_t.reshape(H, t).T
    dcum = dcum[:, :H] - dstep * dt
    db = db + cols_dot(weighted, leave)
    dweighted = dot(acts[:, DI : DI + N], leave)
    dx = dx + dweighted * factor_wide
    to_end = jnp.exp(cum[-1:] - cum)
    dfactor = head_sums(dweighted * x)
    dstep = dstep + dfactor * to_end
    dend = dfactor * dt * to_end
    at_total = head_sums(jnp.sum(leave.astype(f32) * incoming.astype(f32), axis=0, keepdims=True))
    last = jnp.sum(dend, axis=0, keepdims=True) + at_total * totals
    is_end = lax.broadcasted_iota(jnp.int32, (t, 1), 0) == t - 1
    dcum = dcum - dend + jnp.where(is_end, last, 0.0)
    drate = rows_dot(lower_triangle(t), dcum, precision=PRECISE)
    rates = -jnp.exp(log_rate)
    dstep = dstep + drate * rates
    grad_alog = jnp.sum(drate * dt, axis=0) * rates[0]
    draw = dstep * jax.nn.sigmoid(projected[:, DI + CH : E].astype(f32) + bias_dt)
    grad_dtb = jnp.sum(draw, axis=0)
    dconv = jnp.concatenate([dx, db, dc], axis=1) * silu_slope(conv)
    dconv = queue.advance(dconv)
    edge = shifted(dconv[:8], "seq", -1)
    grad_cb = jnp.sum(dconv, axis=0)
    grad_cw = jnp.stack([jnp.sum(dconv * padded[k : k + t].astype(f32), axis=0) for k in range(CONVK)])
    ext = jnp.concatenate([dconv, edge[: CONVK - 1]], axis=0)
    dxbc = jnp.zeros((t, CH), f32)
    for k in range(CONVK):
        dxbc = dxbc + conv_w[k : k + 1] * ext[CONVK - 1 - k : CONVK - 1 - k + t]
    dxbc = dxbc.astype(bf16)
    draw = draw.astype(bf16)
    late = rows_dot(un, jnp.concatenate([dxbc, draw], axis=1)).astype(bf16)
    late_sum = queue.add(late.reshape(count, -1, CH + H), False)
    dxbc = queue.advance(dxbc)
    filler = jnp.zeros((t, w_in.shape[1] - E), bf16)
    dun = cols_dot(jnp.concatenate([dz, dxbc, draw, filler], axis=1), w_in)
    grad_norm_gain = jnp.sum(dun * normed, axis=0)
    dnorm = dun * norm_g
    grad_u = grad_v.astype(f32) + inv_rms * (dnorm - normed * jnp.mean(dnorm * normed, axis=-1, keepdims=True))
    heads = jnp.concatenate([grad_dtb, grad_alog, grad_skip])
    rest = jnp.concatenate(
        [
            grad_cw.reshape(CONVK, count, -1).transpose(1, 0, 2).reshape(count, -1),
            grad_cb.reshape(count, -1),
            grad_norm_gain.reshape(count, -1),
            grad_gate_gain.reshape(count, -1),
            jnp.broadcast_to(heads[None], (count, 3 * H)),
        ],
        axis=1,
    )
    rest_sum = queue.add(rest[:, None], False, f32)
    return grad_u, (early_sum, late_sum, rest_sum)


def body(tokens, cotangent, in_weight, out_weight, conv_weight, conv_bias, norm_gain, gate_gain, dt_bias, a_log, d_skip):
    first = lax.axis_index("section") == 0
    share_count = lax.axis_size("dp") * lax.axis_size("seq")

    def pick(a, b):
        return jnp.where(first, a, b)

    small = jnp.concatenate([conv_weight[0].reshape(-1), conv_bias[0], norm_gain[0], gate_gain[0]])
    rows = in_weight.shape[1]
    extra = -E % 128
    small_count = small.shape[0]
    while rows * extra < small_count:
        extra += 128
    small = jnp.pad(small, (0, rows * extra - small_count)).reshape(rows, extra)
    mine = (jnp.concatenate([in_weight[0], small], axis=1), out_weight[0])
    theirs = tuple(swapped(w) for w in mine)
    heads = jnp.stack([dt_bias[0], a_log[0], d_skip[0]])
    other_heads = swapped(heads)
    head_params = (pick(heads, other_heads), pick(other_heads, heads))
    c_loc, n_loc, g_loc = conv_bias.shape[1], norm_gain.shape[1], gate_gain.shape[1]
    gathered = []
    for layer in range(2):
        shards = tuple(pick(m, o) if layer == 0 else pick(o, m) for m, o in zip(mine, theirs))
        gathered.append(tuple(lax.all_gather(s, WEIGHT_AXES, axis=0, tiled=True) for s in shards))

    def unpacked(layer, w_in, w_out):
        own = w_in[:, E:].reshape(share_count, rows * extra)[:, :small_count].astype(f32)
        cuts = [0, CONVK * c_loc, CONVK * c_loc + c_loc, CONVK * c_loc + c_loc + n_loc]
        conv_w = own[:, : cuts[1]].reshape(share_count, CONVK, c_loc).transpose(1, 0, 2).reshape(CONVK, CH)
        conv_b = own[:, cuts[1] : cuts[2]].reshape(1, CH)
        norm_g = own[:, cuts[2] : cuts[3]].reshape(1, D)
        gate_g = own[:, cuts[3] :].reshape(1, DI)
        hp = head_params[layer]
        return (w_in, w_out, conv_w, conv_b, norm_g, gate_g, hp[0:1], hp[1:2], hp[2:3])

    stream = pick(tokens[0, 0], tokens[1, 0])
    acts, kept, weights = [], [], []
    for layer in range(2):
        if layer == 0:
            weights.append(unpacked(0, *gathered[0]))
            stream, saved, (next_in,) = layer_forward(stream, weights[0], (gathered[1][0],))
        else:
            weights.append(unpacked(1, next_in, gathered[1][1]))
            stream, saved, _ = layer_forward(stream, weights[1])
        acts.append(stream)
        kept.append(saved)
    grad = pick(cotangent[0, 0], cotangent[1, 0])
    grads, sums = [None, None], [None, None]
    queue = Queue()
    for layer in (1, 0):
        grad, sums[layer] = layer_backward(grad, kept[layer], weights[layer], queue)
        grads[layer] = grad
        grad = grad.astype(bf16)
        if layer == 1:
            grad = queue.advance(grad)
    queue.finish()

    def finish(low, high):
        own = pick(low, high)
        return own, swapped(pick(high, low))

    def by_micro(low, high):
        own, other = finish(low, high)
        return jnp.stack([pick(own, other), pick(other, own)])[None, :, None]

    act_out = by_micro(*acts)
    grad_out = by_micro(*grads)
    shares = []
    for low, high in zip(*sums):
        own = pick(low.value[0], high.value[0])
        other = swapped(pick(high.value[0], low.value[0]).astype(low.wire))
        shares.append(own + other.astype(f32))
    early, late, rest = shares
    wout = jnp.concatenate([early[:, :D], early[:, D : 2 * D]], axis=0)
    rest = rest[0]
    parts, start = [], 0
    for size in [CONVK * c_loc, c_loc, n_loc, g_loc, H, H, H]:
        parts.append(rest[start : start + size])
        start += size
    return (
        act_out,
        grad_out,
        jnp.concatenate([early[:, 2 * D :], late], axis=1)[None],
        wout[None],
        parts[0].reshape(CONVK, c_loc)[None],
        parts[1][None],
        parts[2][None],
        parts[3][None],
        parts[4][None],
        parts[5][None],
        parts[6][None],
    )


def solution(mesh):
    in_specs = (
        P(None, "dp", "seq", None),
        P(None, "dp", "seq", None),
        P("section", ("dp", "seq"), None),
        P("section", ("dp", "seq"), None),
        P("section", None, ("dp", "seq")),
        P("section", ("dp", "seq")),
        P("section", ("dp", "seq")),
        P("section", ("dp", "seq")),
        P("section", None),
        P("section", None),
        P("section", None),
    )
    out_specs = (
        P("section", None, "dp", "seq", None),
        P("section", None, "dp", "seq", None),
        P("section", ("dp", "seq"), None),
        P("section", ("dp", "seq"), None),
        P("section", None, ("dp", "seq")),
        P("section", ("dp", "seq")),
        P("section", ("dp", "seq")),
        P("section", ("dp", "seq")),
        P("section", None),
        P("section", None),
        P("section", None),
    )
    return jax.shard_map(body, mesh=mesh, in_specs=in_specs, out_specs=out_specs, check_vma=False)
```
